32 devices in a mesh: grp: 2 (over y), exp: 4 (over z), col: 4 (over x, core).
Axes of the slice: x: 2, y: 2, z: 4, core: 2. Of those that a mesh axis runs over, the one named last changes fastest.
Arguments:
- weights: bfloat16 [24, 768, 4096], P(('grp', 'exp'), None, 'col'), parts along dimension 0, may hold values from -6 to 6
- fisher: bfloat16 [24, 768], P(('grp', 'exp')), parts along dimension 0, may hold values from 0.5 to 2
- members: int32 [24, 4], P('grp'), parts along dimension 0, may hold values from 0 to 1, as said below
- sketch: bfloat16 [24, 4096, 128], P(('grp', 'exp'), 'col'), parts along dimension 0, may hold values from -6 to 6
Outputs:
- base: bfloat16 [8, 768, 4096], P('grp', 'exp', 'col'), parts along dimension 0
- basis: bfloat16 [24, 768, 128], P(('grp', 'exp')), parts along dimension 0
- coeff: bfloat16 [24, 128, 4096], P(('grp', 'exp'), None, 'col'), parts along dimension 0
The draws below stay inside these ranges and needn't reach their ends.
There are 2 independent parts, one for each index of `grp`. The reference program is written for one: setup_inputs(seed, part) draws one part's arguments, and reference() takes and returns one part's arrays. A program takes and returns all parts, laid end to end along the dimension named above; each array names one. Nothing has to cross between parts.
Inputs may be any that keep to these rules, and one draw needn't show every extreme that they name: `members`: each row holds a single 1; every cluster has 2 or more experts.
All inputs are finite; a program needn't handle non-finite values.
Results may differ from the reference program's by a relative error of at most 0.0077.
Values may be sent and summed in bfloat16 or wider, within the bound.
No kernel may reach another device: no remote copies, remote signals or barrier semaphores. Data moves between devices by JAX's collectives and lax.ppermute only.
A program may use at most 128 MiB of HBM per device.

```python
import math
import jax
import jax.numpy as jnp
from jax import lax

D = 4096
UNITS = 768
RANK = 128
EXPERTS = 12
CLUSTERS = 4
N_EXP = 4


def draw_members(key, part):
    key = jax.random.fold_in(key, 7)
    key_one, key_two, key_three, key_four = jax.random.split(key, 4)
    labels = jnp.concatenate([jax.random.permutation(key_one, CLUSTERS), jax.random.permutation(key_two, CLUSTERS), jax.random.randint(key_three, (EXPERTS - 2 * CLUSTERS,), 0, CLUSTERS)]).astype(jnp.int32)
    ordering = jax.random.permutation(key_four, EXPERTS)
    labels = labels[ordering]
    return (labels[:, None] == jnp.arange(CLUSTERS, dtype=jnp.int32)[None, :]).astype(jnp.int32)


def shard_levels(own_key, extent, cuts, least, largest):
    def one(axis_at, blocks):
        heights = jax.random.uniform(jax.random.fold_in(jax.random.fold_in(own_key, 6), axis_at), (blocks,), jnp.float32, least / len(cuts), largest / len(cuts))
        return jnp.repeat(jnp.exp(heights), extent[axis_at] // blocks).reshape((-1,) + (1,) * (len(extent) - axis_at - 1))

    gain = one(*cuts[0])
    for cut in cuts[1:]:
        gain = gain * one(*cut)
    return gain


def scatter_about(rng, extent, scale, bound, shards=(), kind=jnp.bfloat16):
    level = shard_levels(rng, extent, shards, -0.22, 0.18) if shards else 1.0
    values = jax.random.normal(rng, extent, jnp.float32) * scale * level
    return jnp.minimum(jnp.maximum(values, -bound), bound).astype(kind)


def setup_inputs(seed: int = 0, part: int = 0) -> dict:
    key_list = jax.random.split(jax.random.key(seed), 5)
    own_keys = jax.random.split(jax.random.fold_in(key_list[4], part), 5)
    weights = scatter_about(own_keys[0], (EXPERTS, UNITS, D), 1.0, 6.0, ((0, 4), (2, 4)))
    fisher = jnp.clip(jnp.exp(math.log(2.0) - 1.3862944 * jax.random.uniform(own_keys[1], (EXPERTS, UNITS), jnp.float32) ** shard_levels(own_keys[1], (EXPERTS, UNITS), ((0, 4),), -0.2, 0.2)), 0.5, 2.0).astype(jnp.bfloat16)
    members = draw_members(jax.random.fold_in(jax.random.fold_in(key_list[4], part), 71), part)
    sketch = scatter_about(own_keys[3], (EXPERTS, D, RANK), 1.0, 6.0, ((0, 4), (1, 4)))
    return {"weights": weights, "fisher": fisher, "members": members, "sketch": sketch}


HIGH = lax.Precision.HIGHEST

def orthonormal(block):
    gram = jnp.dot(block.T.astype(jnp.float32), block.astype(jnp.float32), precision=HIGH, preferred_element_type=jnp.float32)
    lower = jnp.linalg.cholesky(gram)
    solved = lax.linalg.triangular_solve(lower, block, left_side=False, lower=True, transpose_a=True)
    return (solved * math.sqrt(UNITS)).astype(jnp.bfloat16)

def reference(weights, fisher, members, sketch):
    member_mask = members.astype(jnp.float32)
    row_count = UNITS // N_EXP
    w_blocks = jnp.moveaxis(weights.reshape(EXPERTS, N_EXP, row_count, D), 1, 0)
    f_blocks = jnp.moveaxis(fisher.reshape(EXPERTS, N_EXP, row_count), 1, 0)

    def merge_block(pair):
        w_rows, f_rows = pair
        f_wide = f_rows.astype(jnp.float32)
        weighted = f_wide[:, :, None] * w_rows.astype(jnp.float32)
        numer = jnp.einsum('ek,erd->krd', member_mask, weighted, precision=HIGH)
        denom = jnp.einsum('ek,er->kr', member_mask, f_wide, precision=HIGH)
        base_rows = (numer / denom[:, :, None]).astype(jnp.bfloat16)
        selected = jnp.einsum('ek,krd->erd', member_mask, lax.optimization_barrier(base_rows).astype(jnp.float32), precision=HIGH)
        delta_rows = (w_rows.astype(jnp.float32) - selected).astype(jnp.bfloat16)
        return (base_rows, delta_rows)
    base_blocks, delta_blocks = lax.map(merge_block, (w_blocks, f_blocks))
    base = jnp.moveaxis(base_blocks, 0, 1).reshape(CLUSTERS, UNITS, D)
    delta = jnp.moveaxis(delta_blocks, 0, 1).reshape(EXPERTS, UNITS, D)

    def expert_range(pair):
        delta_one, sketch_one = pair
        first = jnp.dot(delta_one.astype(jnp.float32), sketch_one.astype(jnp.float32), preferred_element_type=jnp.float32)
        range_zero = orthonormal(first)
        back = jnp.dot(delta_one.T.astype(jnp.float32), range_zero.astype(jnp.float32), preferred_element_type=jnp.float32).astype(jnp.bfloat16)
        second = jnp.dot(delta_one.astype(jnp.float32), back.astype(jnp.float32), preferred_element_type=jnp.float32)
        basis_one = orthonormal(second)
        coeff_one = (jnp.dot(basis_one.T.astype(jnp.float32), delta_one.astype(jnp.float32), preferred_element_type=jnp.float32) / math.sqrt(UNITS)).astype(jnp.bfloat16)
        return (basis_one, coeff_one)
    basis, coeff = lax.map(expert_range, (delta, sketch))
    return (base, basis, coeff)
```

```python
import functools
import math

import jax
import jax.numpy as jnp
from jax import lax
from jax.experimental import pallas as pl
from jax.experimental.pallas import tpu as pltpu
from jax.sharding import PartitionSpec as P

HIGH = lax.Precision.HIGHEST
UNIT = 32
VMEM_LIMIT = 48 * 1024 * 1024
SMEM = pl.BlockSpec(memory_space=pltpu.SMEM)


def params():
    return pltpu.CompilerParams(vmem_limit_bytes=VMEM_LIMIT)


def sums_kernel(mask, w_ref, a_ref, f_ref, out_ref):
    experts, rows, cols = w_ref.shape
    clusters = out_ref.shape[0]
    strip, width = 16, 512
    for r in range(0, rows, strip):
        for c in range(0, cols, width):
            totals = [jnp.zeros((strip, width), jnp.float32) for _ in range(clusters)]
            for e in range(2 * experts):
                source = w_ref if e < experts else a_ref
                block = source[e % experts, r : r + strip, c : c + width].astype(jnp.float32)
                block = block * f_ref[r : r + strip, e : e + 1]
                for k in range(clusters):
                    totals[k] = totals[k] + block * mask[e, k]
            for k in range(clusters):
                out_ref[k, r : r + strip, c : c + width] = totals[k].astype(jnp.bfloat16)


def cluster_sums(mask, weights, arrived, fcols, start, rows):
    experts, _, cols = weights.shape
    clusters = mask.shape[1]
    first = start // UNIT
    return pl.pallas_call(
        sums_kernel,
        grid=(rows // UNIT,),
        in_specs=[
            SMEM,
            pl.BlockSpec((experts, UNIT, cols), lambda i: (0, first + i, 0)),
            pl.BlockSpec((experts, UNIT, cols), lambda i: (0, i, 0)),
            pl.BlockSpec((UNIT, fcols.shape[1]), lambda i: (first + i, 0)),
        ],
        out_specs=pl.BlockSpec((clusters, UNIT, cols), lambda i: (0, i, 0)),
        out_shape=jax.ShapeDtypeStruct((clusters, rows, cols), jnp.bfloat16),
        compiler_params=params(),
    )(mask, weights, arrived, fcols)


def base_kernel(p_ref, q_ref, d_ref, out_ref):
    clusters, rows, cols = p_ref.shape
    scale = 1.0 / d_ref[...]
    for k in range(clusters):
        total = p_ref[k].astype(jnp.float32) + q_ref[k].astype(jnp.float32)
        out_ref[k] = (total * scale[:, k : k + 1]).astype(jnp.bfloat16)


def make_base(mine, other, denom, start):
    clusters, rows, cols = mine.shape
    first = start // UNIT
    block = pl.BlockSpec((clusters, UNIT, cols), lambda i: (0, i, 0))
    return pl.pallas_call(
        base_kernel,
        grid=(rows // UNIT,),
        in_specs=[block, block, pl.BlockSpec((UNIT, clusters), lambda i: (first + i, 0))],
        out_specs=block,
        out_shape=jax.ShapeDtypeStruct(mine.shape, jnp.bfloat16),
        compiler_params=params(),
    )(mine, other, denom)


def residual_kernel(meta, w_ref, b_ref, r_ref, s_ref, *refs):
    delta_ref, base_ref, first_ref = refs[-3:]
    experts = w_ref.shape[0]
    inner = meta[experts] == 1

    @pl.when(inner)
    def _():
        base_ref[...] = b_ref[...]

    @pl.when(jnp.logical_not(inner))
    def _():
        base_ref[...] = r_ref[...]

    for e in range(experts):
        chosen = base_ref[meta[e]].astype(jnp.float32)
        delta = (w_ref[e].astype(jnp.float32) - chosen).astype(jnp.bfloat16)
        delta_ref[e] = delta
        first_ref[e] = jnp.dot(delta, s_ref[e], preferred_element_type=jnp.float32)


def residual_chunk(meta, weights, base, arrived, sketch, start, held):
    experts, units, cols = weights.shape
    clusters, rows, _ = base.shape
    rank = sketch.shape[2]
    first = start // UNIT
    chunk = pl.BlockSpec((clusters, UNIT, cols), lambda i: (0, i, 0))
    placed = lambda lead: pl.BlockSpec((lead, UNIT, cols), lambda i: (0, first + i, 0))
    return pl.pallas_call(
        residual_kernel,
        grid=(rows // UNIT,),
        in_specs=[
            SMEM,
            placed(experts),
            chunk,
            chunk,
            pl.BlockSpec(sketch.shape, lambda i: (0, 0, 0)),
        ]
        + [pl.BlockSpec(memory_space=pl.ANY)] * len(held),
        out_specs=[
            placed(experts),
            placed(clusters),
            pl.BlockSpec((experts, UNIT, rank), lambda i: (0, i, 0)),
        ],
        out_shape=[
            jax.ShapeDtypeStruct((experts, units, cols), jnp.bfloat16),
            jax.ShapeDtypeStruct((clusters, units, cols), jnp.bfloat16),
            jax.ShapeDtypeStruct((experts, rows, rank), jnp.float32),
        ],
        input_output_aliases={5 + i: i for i in range(len(held))},
        compiler_params=params(),
    )(meta, weights, base, arrived, sketch, *held)


PIVOTS = 2
GROUP = 8


def inverse_factors(grams):
    size = grams[0].shape[0]
    lane = lax.broadcasted_iota(jnp.int32, (1, size), 1)
    sub = lax.broadcasted_iota(jnp.int32, (GROUP, 1), 0)
    groups = range(size // GROUP)
    tables = [[g[i * GROUP : (i + 1) * GROUP] for i in groups] for g in grams]
    scales = [[jnp.ones((GROUP, size), jnp.float32) for _ in groups] for _ in grams]
    for j in range(0, size, PIVOTS):
        at, offset = divmod(j, GROUP)
        live = range(at, size // GROUP)
        for table, scale in zip(tables, scales):
            cols = [
                {i: jnp.broadcast_to(table[i][:, j + t : j + t + 1], (GROUP, size)) for i in live}
                for t in range(PIVOTS)
            ]
            rows = [table[at][offset + t : offset + t + 1] for t in range(PIVOTS)]
            factors = []
            for t in range(PIVOTS):
                o = offset + t
                pivot = cols[t][at][o : o + 1]
                scale[at] = jnp.where(sub == o, pivot, scale[at])
                inverse = 1.0 / pivot
                factor = {i: cols[t][i] * inverse for i in live}
                factor[at] = jnp.where(sub > o, factor[at], 0.0)
                rows[t] = jnp.where(lane == j + t, 1.0, rows[t])
                for s in range(t + 1, PIVOTS):
                    head = cols[s][at][o : o + 1]
                    for i in live:
                        cols[s][i] = cols[s][i] - factor[i] * head
                    below = factor[at][offset + s : offset + s + 1]
                    rows[s] = jnp.where(lane == j + t, 0.0, rows[s]) - below * rows[t]
                factors.append(factor)
            for i in live:
                value = table[i]
                for t in range(PIVOTS):
                    o = offset + t
                    here = lane == j + t
                    if i == at:
                        value = jnp.where(here & (sub > o), 0.0, value)
                        value = jnp.where(here & (sub == o), 1.0, value)
                    else:
                        value = jnp.where(here, 0.0, value)
                    value = value - factors[t][i] * rows[t]
                table[i] = value
    out = []
    for table, scale in zip(tables, scales):
        parts = []
        for i in groups:
            keep = lane <= sub + i * GROUP
            parts.append(jnp.where(keep, table[i] * lax.rsqrt(scale[i]), 0.0))
        out.append(jnp.concatenate(parts, axis=0))
    return out


def contract(left, right, dims, precision=None):
    return lax.dot_general(
        left, right, (dims, ((), ())), precision=precision, preferred_element_type=jnp.float32
    )


def ranges(values, units):
    grams = [contract(y, y, ((0,), (0,)), HIGH) for y in values]
    factors = inverse_factors(grams)
    return [
        (contract(y, m, ((1,), (1,)), HIGH) * math.sqrt(units)).astype(jnp.bfloat16)
        for y, m in zip(values, factors)
    ]


def power_kernel(y_ref, delta_ref, second_ref, held, sem):
    experts, units, _ = y_ref.shape
    copy = pltpu.make_async_copy(delta_ref, held, sem)
    copy.start()
    start = ranges([y_ref[e] for e in range(experts)], units)
    copy.wait()
    for e in range(experts):
        back = contract(start[e], held[e], ((0,), (0,))).astype(jnp.bfloat16)
        second_ref[e] = contract(held[e], back, ((1,), (1,)))


def power_step(summed, delta):
    return pl.pallas_call(
        power_kernel,
        in_specs=[pl.BlockSpec(memory_space=pltpu.VMEM), pl.BlockSpec(memory_space=pl.ANY)],
        out_specs=pl.BlockSpec(memory_space=pltpu.VMEM),
        out_shape=jax.ShapeDtypeStruct(summed.shape, jnp.float32),
        scratch_shapes=[pltpu.VMEM(delta.shape, jnp.bfloat16), pltpu.SemaphoreType.DMA],
        compiler_params=params(),
    )(summed, delta)


def project_kernel(y_ref, delta_ref, basis_ref, coeff_ref, held, sem):
    experts, units, _ = y_ref.shape
    copy = pltpu.make_async_copy(delta_ref, held, sem)
    copy.start()
    basis = ranges([y_ref[e] for e in range(experts)], units)
    copy.wait()
    for e in range(experts):
        basis_ref[e] = basis[e]
        coeff = contract(basis[e], held[e], ((0,), (0,)))
        coeff_ref[e] = (coeff * (1.0 / math.sqrt(units))).astype(jnp.bfloat16)


def project(summed, delta):
    experts, units, rank = summed.shape
    return pl.pallas_call(
        project_kernel,
        in_specs=[pl.BlockSpec(memory_space=pltpu.VMEM), pl.BlockSpec(memory_space=pl.ANY)],
        out_specs=[pl.BlockSpec(memory_space=pltpu.VMEM)] * 2,
        out_shape=[
            jax.ShapeDtypeStruct(summed.shape, jnp.bfloat16),
            jax.ShapeDtypeStruct((experts, rank, delta.shape[2]), jnp.bfloat16),
        ],
        scratch_shapes=[pltpu.VMEM(delta.shape, jnp.bfloat16), pltpu.SemaphoreType.DMA],
        compiler_params=params(),
    )(summed, delta)


def sum_columns(value, size):
    bit = 1
    while bit < size:
        pairs = [(i, i ^ bit) for i in range(size)]
        value = value + lax.ppermute(value, "col", pairs)
        bit *= 2
    return value


def merge_folded(weights, fisher, member_mask, sketch, col_size):
    inwards, across, outwards = [(0, 1), (3, 2)], [(1, 2), (2, 1)], [(1, 0), (2, 3)]
    experts, units, cols = weights.shape
    clusters = member_mask.shape[1]
    place = lax.axis_index("exp")
    inner = ((place == 1) | (place == 2)).astype(jnp.int32)
    mine = lax.dynamic_slice_in_dim(member_mask, place * experts, experts)
    partner = lax.dynamic_slice_in_dim(member_mask, (place ^ 1) * experts, experts)
    mask = jnp.concatenate([mine, partner], axis=0)
    labels = jnp.argmax(mine, axis=1).astype(jnp.int32)
    meta = jnp.concatenate([labels, inner[None]])
    fcols = jnp.concatenate([fisher, lax.ppermute(fisher, "exp", inwards)], axis=0)
    fcols = fcols.astype(jnp.float32).T
    half = jnp.sum(fcols[:, :, None] * mask[None], axis=1)
    denom = half + lax.ppermute(half, "exp", across)

    sizes = [1, 2, 3, 3, 3, 3, 3, 3, 2, 1]
    starts = [UNIT * sum(sizes[:c]) for c in range(len(sizes))]
    held, firsts = (), []
    for start, size in zip(starts, sizes):
        rows = size * UNIT
        arrived = lax.ppermute(weights[:, start : start + rows], "exp", inwards)
        sums = cluster_sums(mask, weights, arrived, fcols, start, rows)
        other = lax.ppermute(sums, "exp", across)
        base = make_base(sums, other, denom, start)
        moved = lax.ppermute(base, "exp", outwards)
        *held, first = residual_chunk(meta, weights, base, moved, sketch, start, held)
        firsts.append(first)
    delta, bases = held
    late = 2
    summed = [
        sum_columns(jnp.concatenate(firsts[:-late], axis=1), col_size),
        sum_columns(jnp.concatenate(firsts[-late:], axis=1), col_size),
    ]
    quarter = units // 4
    base = lax.dynamic_slice_in_dim(bases, place * quarter, quarter, axis=1)
    return base, delta, jnp.concatenate(summed, axis=1)


def merge_spread(weights, fisher, member_mask, sketch, col_size):
    moved = lax.all_to_all(weights, "exp", split_axis=1, concat_axis=0, tiled=True)
    f_rows = lax.all_to_all(fisher, "exp", split_axis=1, concat_axis=0, tiled=True)
    f_wide = f_rows.astype(jnp.float32)
    weighted = f_wide[:, :, None] * moved.astype(jnp.float32)
    numer = jnp.einsum("ek,erc->krc", member_mask, weighted, precision=HIGH)
    denom = jnp.einsum("ek,er->kr", member_mask, f_wide, precision=HIGH)
    base = (numer / denom[:, :, None]).astype(jnp.bfloat16)
    chosen = jnp.take(base, jnp.argmax(member_mask, axis=1), axis=0)
    residual = (moved.astype(jnp.float32) - chosen.astype(jnp.float32)).astype(jnp.bfloat16)
    delta = lax.all_to_all(residual, "exp", split_axis=0, concat_axis=1, tiled=True)
    first = jnp.einsum("nrc,nck->nrk", delta, sketch, preferred_element_type=jnp.float32)
    return base, delta, sum_columns(first, col_size)


def body(exp_size, col_size, weights, fisher, members, sketch):
    member_mask = members.astype(jnp.float32)
    merge = merge_folded if exp_size == 4 else merge_spread
    base, delta, first = merge(weights, fisher, member_mask, sketch, col_size)
    second = sum_columns(power_step(first, delta), col_size)
    basis, coeff = project(second, delta)
    return base, basis, coeff


def solution(mesh):
    in_specs = (
        P(("grp", "exp"), None, "col"),
        P(("grp", "exp"), None),
        P("grp", None),
        P(("grp", "exp"), "col", None),
    )
    out_specs = (
        P("grp", "exp", "col"),
        P(("grp", "exp"), None, None),
        P(("grp", "exp"), None, "col"),
    )
    run = functools.partial(body, mesh.shape["exp"], mesh.shape["col"])
    return jax.shard_map(run, mesh=mesh, in_specs=in_specs, out_specs=out_specs, check_vma=False)
```

```python
import functools
import math

import jax
import jax.numpy as jnp
from jax import lax
from jax.experimental import pallas as pl
from jax.experimental.pallas import tpu as pltpu
from jax.sharding import PartitionSpec as P

HIGH = lax.Precision.HIGHEST
UNIT = 32
VMEM_LIMIT = 48 * 1024 * 1024
SMEM = pl.BlockSpec(memory_space=pltpu.SMEM)


def params():
    return pltpu.CompilerParams(vmem_limit_bytes=VMEM_LIMIT)


def sums_kernel(mask, w_ref, a_ref, f_ref, *refs):
    out_ref = refs[-1]
    experts, rows, cols = w_ref.shape
    clusters = out_ref.shape[0]
    strip, width = 16, 512
    for r in range(0, rows, strip):
        for c in range(0, cols, width):
            totals = [jnp.zeros((strip, width), jnp.float32) for _ in range(clusters)]
            for e in range(2 * experts):
                source = w_ref if e < experts else a_ref
                block = source[e % experts, r : r + strip, c : c + width].astype(jnp.float32)
                block = block * f_ref[r : r + strip, e : e + 1]
                for k in range(clusters):
                    totals[k] = totals[k] + block * mask[e, k]
            for k in range(clusters):
                out_ref[k, r : r + strip, c : c + width] = totals[k].astype(jnp.bfloat16)


ANY = pl.BlockSpec(memory_space=pl.ANY)


def cluster_sums(mask, weights, arrived, fcols, start, rows, after):
    experts, _, cols = weights.shape
    clusters = mask.shape[1]
    first = start // UNIT
    return pl.pallas_call(
        sums_kernel,
        grid=(rows // UNIT,),
        in_specs=[
            SMEM,
            pl.BlockSpec((experts, UNIT, cols), lambda i: (0, first + i, 0)),
            pl.BlockSpec((experts, UNIT, cols), lambda i: (0, i, 0)),
            pl.BlockSpec((UNIT, fcols.shape[1]), lambda i: (first + i, 0)),
        ]
        + [ANY] * len(after),
        out_specs=pl.BlockSpec((clusters, UNIT, cols), lambda i: (0, i, 0)),
        out_shape=jax.ShapeDtypeStruct((clusters, rows, cols), jnp.bfloat16),
        compiler_params=params(),
    )(mask, weights, arrived, fcols, *after)


def base_kernel(p_ref, q_ref, d_ref, *refs):
    out_ref = refs[-1]
    clusters, rows, cols = p_ref.shape
    scale = 1.0 / d_ref[...]
    for k in range(clusters):
        total = p_ref[k].astype(jnp.float32) + q_ref[k].astype(jnp.float32)
        out_ref[k] = (total * scale[:, k : k + 1]).astype(jnp.bfloat16)


def make_base(mine, other, denom, start, after):
    clusters, rows, cols = mine.shape
    first = start // UNIT
    block = pl.BlockSpec((clusters, UNIT, cols), lambda i: (0, i, 0))
    return pl.pallas_call(
        base_kernel,
        grid=(rows // UNIT,),
        in_specs=[block, block, pl.BlockSpec((UNIT, clusters), lambda i: (first + i, 0))]
        + [ANY] * len(after),
        out_specs=block,
        out_shape=jax.ShapeDtypeStruct(mine.shape, jnp.bfloat16),
        compiler_params=params(),
    )(mine, other, denom, *after)


def residual_kernel(meta, w_ref, b_ref, r_ref, s_ref, *refs):
    delta_ref, base_ref, first_ref = refs[-3:]
    experts = w_ref.shape[0]
    inner = meta[experts] == 1

    @pl.when(inner)
    def _():
        base_ref[...] = b_ref[...]

    @pl.when(jnp.logical_not(inner))
    def _():
        base_ref[...] = r_ref[...]

    for e in range(experts):
        chosen = base_ref[meta[e]].astype(jnp.float32)
        delta = (w_ref[e].astype(jnp.float32) - chosen).astype(jnp.bfloat16)
        delta_ref[e] = delta
        first_ref[e] = jnp.dot(delta, s_ref[e], preferred_element_type=jnp.float32)


def residual_chunk(meta, weights, base, arrived, sketch, start, held, after):
    experts, units, cols = weights.shape
    clusters, rows, _ = base.shape
    rank = sketch.shape[2]
    first = start // UNIT
    chunk = pl.BlockSpec((clusters, UNIT, cols), lambda i: (0, i, 0))
    placed = lambda lead: pl.BlockSpec((lead, UNIT, cols), lambda i: (0, first + i, 0))
    return pl.pallas_call(
        residual_kernel,
        grid=(rows // UNIT,),
        in_specs=[
            SMEM,
            placed(experts),
            chunk,
            chunk,
            pl.BlockSpec(sketch.shape, lambda i: (0, 0, 0)),
        ]
        + [ANY] * (len(held) + len(after)),
        out_specs=[
            placed(experts),
            placed(clusters),
            pl.BlockSpec((experts, UNIT, rank), lambda i: (0, i, 0)),
        ],
        out_shape=[
            jax.ShapeDtypeStruct((experts, units, cols), jnp.bfloat16),
            jax.ShapeDtypeStruct((clusters, units, cols), jnp.bfloat16),
            jax.ShapeDtypeStruct((experts, rows, rank), jnp.float32),
        ],
        input_output_aliases={5 + i: i for i in range(len(held))},
        compiler_params=params(),
    )(meta, weights, base, arrived, sketch, *held, *after)


PIVOTS = 2
GROUP = 8


def inverse_factors(grams):
    size = grams[0].shape[0]
    lane = lax.broadcasted_iota(jnp.int32, (1, size), 1)
    sub = lax.broadcasted_iota(jnp.int32, (GROUP, 1), 0)
    groups = range(size // GROUP)
    tables = [[g[i * GROUP : (i + 1) * GROUP] for i in groups] for g in grams]
    scales = [[jnp.ones((GROUP, size), jnp.float32) for _ in groups] for _ in grams]
    for j in range(0, size, PIVOTS):
        at, offset = divmod(j, GROUP)
        live = range(at, size // GROUP)
        for table, scale in zip(tables, scales):
            cols = [
                {i: jnp.broadcast_to(table[i][:, j + t : j + t + 1], (GROUP, size)) for i in live}
                for t in range(PIVOTS)
            ]
            rows = [table[at][offset + t : offset + t + 1] for t in range(PIVOTS)]
            factors = []
            for t in range(PIVOTS):
                o = offset + t
                pivot = cols[t][at][o : o + 1]
                scale[at] = jnp.where(sub == o, pivot, scale[at])
                inverse = 1.0 / pivot
                factor = {i: cols[t][i] * inverse for i in live}
                factor[at] = jnp.where(sub > o, factor[at], 0.0)
                rows[t] = jnp.where(lane == j + t, 1.0, rows[t])
                for s in range(t + 1, PIVOTS):
                    head = cols[s][at][o : o + 1]
                    for i in live:
                        cols[s][i] = cols[s][i] - factor[i] * head
                    below = factor[at][offset + s : offset + s + 1]
                    rows[s] = jnp.where(lane == j + t, 0.0, rows[s]) - below * rows[t]
                factors.append(factor)
            for i in live:
                value = table[i]
                for t in range(PIVOTS):
                    o = offset + t
                    here = lane == j + t
                    if i == at:
                        value = jnp.where(here & (sub > o), 0.0, value)
                        value = jnp.where(here & (sub == o), 1.0, value)
                    else:
                        value = jnp.where(here, 0.0, value)
                    value = value - factors[t][i] * rows[t]
                table[i] = value
    out = []
    for table, scale in zip(tables, scales):
        parts = []
        for i in groups:
            keep = lane <= sub + i * GROUP
            parts.append(jnp.where(keep, table[i] * lax.rsqrt(scale[i]), 0.0))
        out.append(jnp.concatenate(parts, axis=0))
    return out


def contract(left, right, dims, precision=None):
    return lax.dot_general(
        left, right, (dims, ((), ())), precision=precision, preferred_element_type=jnp.float32
    )


def ranges(values, units):
    grams = [contract(y, y, ((0,), (0,)), HIGH) for y in values]
    factors = inverse_factors(grams)
    return [
        (contract(y, m, ((1,), (1,)), HIGH) * math.sqrt(units)).astype(jnp.bfloat16)
        for y, m in zip(values, factors)
    ]


def power_kernel(side, y_ref, delta_ref, keep_ref, send_ref, held, sem):
    experts, units, _ = y_ref.shape
    half = units // 2
    copy = pltpu.make_async_copy(delta_ref, held, sem)
    copy.start()
    start = ranges([y_ref[e] for e in range(experts)], units)
    copy.wait()
    own = pl.multiple_of(side[0] * half, half)
    other = pl.multiple_of((1 - side[0]) * half, half)
    for e in range(experts):
        back = contract(start[e], held[e], ((0,), (0,))).astype(jnp.bfloat16)
        keep_ref[e] = contract(held[e, pl.ds(own, half)], back, ((1,), (1,)))
        send_ref[e] = contract(held[e, pl.ds(other, half)], back, ((1,), (1,)))


def power_step(side, summed, delta):
    experts, units, rank = summed.shape
    part = jax.ShapeDtypeStruct((experts, units // 2, rank), jnp.float32)
    return pl.pallas_call(
        power_kernel,
        in_specs=[SMEM, pl.BlockSpec(memory_space=pltpu.VMEM), ANY],
        out_specs=[pl.BlockSpec(memory_space=pltpu.VMEM)] * 2,
        out_shape=[part, part],
        scratch_shapes=[pltpu.VMEM(delta.shape, jnp.bfloat16), pltpu.SemaphoreType.DMA],
        compiler_params=params(),
    )(side, summed, delta)


def project_kernel(side, *refs):
    parts, (delta_ref, basis_ref, coeff_ref, value, held, sem) = refs[:-6], refs[-6:]
    experts, half, _ = parts[0].shape
    units = 2 * half
    copy = pltpu.make_async_copy(delta_ref, held, sem)
    copy.start()
    count = len(parts) // 2
    for place, group in ((side[0], parts[:count]), (1 - side[0], parts[count:])):
        total = group[0][...].astype(jnp.float32)
        for part in group[1:]:
            total = total + part[...].astype(jnp.float32)
        value[:, pl.ds(pl.multiple_of(place * half, half), half)] = total
    basis = ranges([value[e] for e in range(experts)], units)
    copy.wait()
    for e in range(experts):
        basis_ref[e] = basis[e]
        coeff = contract(basis[e], held[e], ((0,), (0,)))
        coeff_ref[e] = (coeff * (1.0 / math.sqrt(units))).astype(jnp.bfloat16)


def project(side, mine, others, delta):
    experts, units, _ = delta.shape
    rank = mine[0].shape[2]
    vmem = pl.BlockSpec(memory_space=pltpu.VMEM)
    return pl.pallas_call(
        project_kernel,
        in_specs=[SMEM] + [vmem] * (len(mine) + len(others)) + [ANY],
        out_specs=[vmem] * 2,
        out_shape=[
            jax.ShapeDtypeStruct((experts, units, rank), jnp.bfloat16),
            jax.ShapeDtypeStruct((experts, rank, delta.shape[2]), jnp.bfloat16),
        ],
        scratch_shapes=[
            pltpu.VMEM((experts, units, rank), jnp.float32),
            pltpu.VMEM(delta.shape, jnp.bfloat16),
            pltpu.SemaphoreType.DMA,
        ],
        compiler_params=params(),
    )(side, *mine, *others, delta)


def swap(value, bit, size):
    return lax.ppermute(value, "col", [(i, i ^ bit) for i in range(size)])


def sum_columns(value, size):
    bit = 1
    while bit < size:
        value = value + swap(value, bit, size)
        bit *= 2
    return value


def sum_halves(keep, send, size):
    total = (keep + swap(send, 1, size)).astype(jnp.bfloat16)
    bit = 2
    while 2 * bit < size:
        total = (total.astype(jnp.float32) + swap(total, bit, size).astype(jnp.float32)).astype(
            jnp.bfloat16
        )
        bit *= 2
    far = swap(total, bit, size)
    return (total, far), (swap(total, 1, size), swap(far, 1, size))


def merge_folded(weights, fisher, member_mask, sketch, col_size):
    inwards, across, outwards = [(0, 1), (3, 2)], [(1, 2), (2, 1)], [(1, 0), (2, 3)]
    experts, units, cols = weights.shape
    clusters = member_mask.shape[1]
    place = lax.axis_index("exp")
    inner = ((place == 1) | (place == 2)).astype(jnp.int32)
    mine = lax.dynamic_slice_in_dim(member_mask, place * experts, experts)
    partner = lax.dynamic_slice_in_dim(member_mask, (place ^ 1) * experts, experts)
    mask = jnp.concatenate([mine, partner], axis=0)
    labels = jnp.argmax(mine, axis=1).astype(jnp.int32)
    meta = jnp.concatenate([labels, inner[None]])
    fcols = jnp.concatenate([fisher, lax.ppermute(fisher, "exp", inwards)], axis=0)
    fcols = fcols.astype(jnp.float32).T
    half = jnp.sum(fcols[:, :, None] * mask[None], axis=1)
    denom = half + lax.ppermute(half, "exp", across)

    sizes = [1, 2, 3, 3, 3, 3, 3, 3, 2, 1]
    starts = [UNIT * sum(sizes[:c]) for c in range(len(sizes))]
    count = len(sizes)
    arrived, sums, others, base, moved, firsts = {}, {}, {}, {}, {}, {}
    held, after = (), ()
    for c in range(count):
        block = weights[:, starts[c] : starts[c] + sizes[c] * UNIT]
        arrived[c] = lax.ppermute(block, "exp", inwards)
    for step in range(count + 2):
        c = step
        if c < count:
            rows = sizes[c] * UNIT
            sums[c] = cluster_sums(mask, weights, arrived[c], fcols, starts[c], rows, after)
            others[c] = lax.ppermute(sums[c], "exp", across)
            after = (sums[c],)
        c = step - 1
        if 0 <= c < count:
            base[c] = make_base(sums[c], others[c], denom, starts[c], after)
            moved[c] = lax.ppermute(base[c], "exp", outwards)
            after = (base[c],)
        c = step - 2
        if 0 <= c < count:
            *held, firsts[c] = residual_chunk(
                meta, weights, base[c], moved[c], sketch, starts[c], held, after
            )
            after = (firsts[c],)
    firsts = [firsts[c] for c in range(count)]
    delta, bases = held
    late = 2
    summed = [
        sum_columns(jnp.concatenate(firsts[:-late], axis=1), col_size),
        sum_columns(jnp.concatenate(firsts[-late:], axis=1), col_size),
    ]
    quarter = units // 4
    base = lax.dynamic_slice_in_dim(bases, place * quarter, quarter, axis=1)
    return base, delta, jnp.concatenate(summed, axis=1)


def merge_spread(weights, fisher, member_mask, sketch, col_size):
    moved = lax.all_to_all(weights, "exp", split_axis=1, concat_axis=0, tiled=True)
    f_rows = lax.all_to_all(fisher, "exp", split_axis=1, concat_axis=0, tiled=True)
    f_wide = f_rows.astype(jnp.float32)
    weighted = f_wide[:, :, None] * moved.astype(jnp.float32)
    numer = jnp.einsum("ek,erc->krc", member_mask, weighted, precision=HIGH)
    denom = jnp.einsum("ek,er->kr", member_mask, f_wide, precision=HIGH)
    base = (numer / denom[:, :, None]).astype(jnp.bfloat16)
    chosen = jnp.take(base, jnp.argmax(member_mask, axis=1), axis=0)
    residual = (moved.astype(jnp.float32) - chosen.astype(jnp.float32)).astype(jnp.bfloat16)
    delta = lax.all_to_all(residual, "exp", split_axis=0, concat_axis=1, tiled=True)
    first = jnp.einsum("nrc,nck->nrk", delta, sketch, preferred_element_type=jnp.float32)
    return base, delta, sum_columns(first, col_size)


def body(exp_size, col_size, weights, fisher, members, sketch):
    member_mask = members.astype(jnp.float32)
    merge = merge_folded if exp_size == 4 else merge_spread
    base, delta, first = merge(weights, fisher, member_mask, sketch, col_size)
    side = lax.rem(lax.axis_index("col"), 2)[None]
    mine, others = sum_halves(*power_step(side, first, delta), col_size)
    basis, coeff = project(side, mine, others, delta)
    return base, basis, coeff


def solution(mesh):
    in_specs = (
        P(("grp", "exp"), None, "col"),
        P(("grp", "exp"), None),
        P("grp", None),
        P(("grp", "exp"), "col", None),
    )
    out_specs = (
        P("grp", "exp", "col"),
        P(("grp", "exp"), None, None),
        P(("grp", "exp"), None, "col"),
    )
    run = functools.partial(body, mesh.shape["exp"], mesh.shape["col"])
    return jax.shard_map(run, mesh=mesh, in_specs=in_specs, out_specs=out_specs, check_vma=False)
```

```python
import functools
import math

import jax
import jax.numpy as jnp
from jax import lax
from jax.experimental import pallas as pl
from jax.experimental.pallas import tpu as pltpu
from jax.sharding import PartitionSpec as P

HIGH = lax.Precision.HIGHEST
UNIT = 32
VMEM_LIMIT = 48 * 1024 * 1024
SMEM = pl.BlockSpec(memory_space=pltpu.SMEM)


def params():
    return pltpu.CompilerParams(vmem_limit_bytes=VMEM_LIMIT)


SMALL = pl.CostEstimate(flops=1, transcendentals=0, bytes_accessed=1)
ANY = pl.BlockSpec(memory_space=pl.ANY)
HBM = pl.BlockSpec(memory_space=pltpu.HBM)


def in_hbm(array):
    return pltpu.with_memory_space_constraint(array, pltpu.HBM)


def sums_kernel(ahead, mask, w_ref, a_ref, f_ref, *refs):
    experts, rows, cols = w_ref.shape
    if ahead:
        out_ref, next_ref = refs[-2:]
        next_ref[...] = refs[0][...]
    else:
        out_ref = refs[-1]
    clusters = out_ref.shape[0]
    strip, width = 16, 512
    for r in range(0, rows, strip):
        for c in range(0, cols, width):
            totals = [jnp.zeros((strip, width), jnp.float32) for _ in range(clusters)]
            for e in range(2 * experts):
                source = w_ref if e < experts else a_ref
                block = source[e % experts, r : r + strip, c : c + width].astype(jnp.float32)
                block = block * f_ref[r : r + strip, e : e + 1]
                for k in range(clusters):
                    totals[k] = totals[k] + block * mask[e, k]
            for k in range(clusters):
                out_ref[k, r : r + strip, c : c + width] = totals[k].astype(jnp.bfloat16)


def cluster_sums(mask, weights, arrived, fcols, start, rows, ahead, after):
    experts, _, cols = weights.shape
    clusters = mask.shape[1]
    first = start // UNIT
    steps = rows // UNIT
    out_specs = [pl.BlockSpec((clusters, UNIT, cols), lambda i: (0, i, 0))]
    out_shape = [jax.ShapeDtypeStruct((clusters, rows, cols), jnp.bfloat16)]
    extra, extra_specs = list(after), [ANY] * len(after)
    if ahead is not None:
        begin, length = ahead
        split = length % (16 * steps) == 0 and begin % (length // steps) == 0
        part = length // steps if split else length
        shape = (experts, part, cols)
        if part != length:
            at = begin // part
            extra_specs.insert(0, pl.BlockSpec(shape, lambda i: (0, at + i, 0)))
            out_specs.append(pl.BlockSpec(shape, lambda i: (0, i, 0)))
        else:
            place = (pl.Element(experts), pl.Element(length), pl.Element(cols))
            extra_specs.insert(0, pl.BlockSpec(place, lambda i: (0, begin, 0)))
            out_specs.append(pl.BlockSpec(shape, lambda i: (0, 0, 0)))
        out_shape.append(jax.ShapeDtypeStruct((experts, length, cols), jnp.bfloat16))
        extra.insert(0, in_hbm(weights))
    return pl.pallas_call(
        functools.partial(sums_kernel, ahead is not None),
        grid=(steps,),
        in_specs=[
            SMEM,
            pl.BlockSpec((experts, UNIT, cols), lambda i: (0, first + i, 0)),
            pl.BlockSpec((experts, UNIT, cols), lambda i: (0, i, 0)),
            pl.BlockSpec((UNIT, fcols.shape[1]), lambda i: (first + i, 0)),
        ]
        + extra_specs,
        out_specs=out_specs,
        out_shape=out_shape,
        cost_estimate=SMALL,
        compiler_params=params(),
    )(mask, in_hbm(weights), arrived, fcols, *extra)


def base_kernel(chosen, p_ref, q_ref, d_ref, *refs):
    clusters, rows, cols = p_ref.shape
    out_ref = refs[-2] if chosen is not None else refs[-1]
    scale = 1.0 / d_ref[...]
    for k in range(clusters):
        total = p_ref[k].astype(jnp.float32) + q_ref[k].astype(jnp.float32)
        out_ref[k] = (total * scale[:, k : k + 1]).astype(jnp.bfloat16)


def chosen_base_kernel(labels, *refs):
    base_kernel(labels, *refs)
    out_ref, chosen_ref = refs[-2:]
    for e in range(chosen_ref.shape[0]):
        chosen_ref[e] = out_ref[labels[e]]


def make_base(mine, other, denom, start, labels, after):
    clusters, rows, cols = mine.shape
    first = start // UNIT
    block = pl.BlockSpec((clusters, UNIT, cols), lambda i: (0, i, 0))
    in_specs = [block, block, pl.BlockSpec((UNIT, clusters), lambda i: (first + i, 0))]
    shape = jax.ShapeDtypeStruct(mine.shape, jnp.bfloat16)
    kernel, operands, outs, shapes = functools.partial(base_kernel, None), (), block, shape
    if labels is not None:
        kernel, operands = chosen_base_kernel, (labels,)
        in_specs = [SMEM] + in_specs
        experts = labels.shape[0]
        outs = [block, pl.BlockSpec((experts, UNIT, cols), lambda i: (0, i, 0))]
        shapes = [shape, jax.ShapeDtypeStruct((experts, rows, cols), jnp.bfloat16)]
    return pl.pallas_call(
        kernel,
        grid=(rows // UNIT,),
        in_specs=in_specs + [ANY] * len(after),
        out_specs=outs,
        out_shape=shapes,
        cost_estimate=SMALL,
        compiler_params=params(),
    )(*operands, mine, other, denom, *after)


def residual_kernel(meta, w_ref, b_ref, r_ref, s_ref, *refs):
    delta_ref, base_ref, first_ref = refs[-3:]
    experts = w_ref.shape[0]
    by_expert = r_ref.shape[0] == experts
    inner = meta[experts] == 1
    base_ref[...] = b_ref[...] if by_expert else r_ref[...]

    def subtract(source, indices):
        for e in range(experts):
            chosen = source[indices[e]].astype(jnp.float32)
            delta_ref[e] = (w_ref[e].astype(jnp.float32) - chosen).astype(jnp.bfloat16)

    labels = [meta[e] for e in range(experts)]

    @pl.when(inner)
    def _():
        if not by_expert:
            base_ref[...] = b_ref[...]
        subtract(b_ref, labels)

    @pl.when(jnp.logical_not(inner))
    def _():
        subtract(r_ref, range(experts) if by_expert else labels)

    for e in range(experts):
        first_ref[e] = jnp.dot(delta_ref[e], s_ref[e], preferred_element_type=jnp.float32)


def residual_chunk(meta, weights, base, arrived, sketch, start, held, after):
    experts, units, cols = weights.shape
    clusters, rows, _ = base.shape
    rank = sketch.shape[2]
    first = start // UNIT
    chunk = lambda lead: pl.BlockSpec((lead, UNIT, cols), lambda i: (0, i, 0))
    placed = lambda lead: pl.BlockSpec((lead, UNIT, cols), lambda i: (0, first + i, 0))
    return pl.pallas_call(
        residual_kernel,
        grid=(rows // UNIT,),
        in_specs=[
            SMEM,
            placed(experts),
            chunk(clusters),
            chunk(arrived.shape[0]),
            pl.BlockSpec(sketch.shape, lambda i: (0, 0, 0)),
        ]
        + [HBM] * len(held)
        + [ANY] * len(after),
        out_specs=[
            placed(experts),
            placed(clusters),
            pl.BlockSpec((experts, UNIT, rank), lambda i: (0, i, 0)),
        ],
        out_shape=[
            pltpu.HBM((experts, units, cols), jnp.bfloat16),
            pltpu.HBM((clusters, units, cols), jnp.bfloat16),
            jax.ShapeDtypeStruct((experts, rows, rank), jnp.float32),
        ],
        cost_estimate=SMALL,
        input_output_aliases={5 + i: i for i in range(len(held))},
        compiler_params=params(),
    )(meta, in_hbm(weights), base, arrived, sketch, *held, *after)


def copy_kernel(place, in_ref, out_ref):
    out_ref[...] = in_ref[...]


def own_quarter(place, bases):
    clusters, units, cols = bases.shape
    block = (clusters, units // 4, cols // 2)
    return pl.pallas_call(
        copy_kernel,
        grid_spec=pltpu.PrefetchScalarGridSpec(
            num_scalar_prefetch=1,
            grid=(2,),
            in_specs=[pl.BlockSpec(block, lambda i, place: (0, place[0], i))],
            out_specs=pl.BlockSpec(block, lambda i, place: (0, 0, i)),
        ),
        out_shape=jax.ShapeDtypeStruct((clusters, units // 4, cols), jnp.bfloat16),
        compiler_params=params(),
    )(place, bases)


PIVOTS = 2
GROUP = 8


def inverse_factors(grams):
    size = grams[0].shape[0]
    lane = lax.broadcasted_iota(jnp.int32, (1, size), 1)
    sub = lax.broadcasted_iota(jnp.int32, (GROUP, 1), 0)
    groups = range(size // GROUP)
    tables = [[g[i * GROUP : (i + 1) * GROUP] for i in groups] for g in grams]
    scales = [[jnp.ones((GROUP, size), jnp.float32) for _ in groups] for _ in grams]
    for j in range(0, size, PIVOTS):
        at, offset = divmod(j, GROUP)
        live = range(at, size // GROUP)
        for table, scale in zip(tables, scales):
            cols = [
                {i: jnp.broadcast_to(table[i][:, j + t : j + t + 1], (GROUP, size)) for i in live}
                for t in range(PIVOTS)
            ]
            rows = [table[at][offset + t : offset + t + 1] for t in range(PIVOTS)]
            factors = []
            for t in range(PIVOTS):
                o = offset + t
                pivot = cols[t][at][o : o + 1]
                scale[at] = jnp.where(sub == o, pivot, scale[at])
                inverse = 1.0 / pivot
                factor = {i: cols[t][i] * inverse for i in live}
                factor[at] = jnp.where(sub > o, factor[at], 0.0)
                rows[t] = jnp.where(lane == j + t, 1.0, rows[t])
                for s in range(t + 1, PIVOTS):
                    head = cols[s][at][o : o + 1]
                    for i in live:
                        cols[s][i] = cols[s][i] - factor[i] * head
                    below = factor[at][offset + s : offset + s + 1]
                    rows[s] = jnp.where(lane == j + t, 0.0, rows[s]) - below * rows[t]
                factors.append(factor)
            for i in live:
                value = table[i]
                for t in range(PIVOTS):
                    o = offset + t
                    here = lane == j + t
                    if i == at:
                        value = jnp.where(here & (sub > o), 0.0, value)
                        value = jnp.where(here & (sub == o), 1.0, value)
                    else:
                        value = jnp.where(here, 0.0, value)
                    value = value - factors[t][i] * rows[t]
                table[i] = value
    out = []
    for table, scale in zip(tables, scales):
        parts = []
        for i in groups:
            keep = lane <= sub + i * GROUP
            parts.append(jnp.where(keep, table[i] * lax.rsqrt(scale[i]), 0.0))
        out.append(jnp.concatenate(parts, axis=0))
    return out


def contract(left, right, dims, precision=None):
    return lax.dot_general(
        left, right, (dims, ((), ())), precision=precision, preferred_element_type=jnp.float32
    )


def ranges(values, units):
    grams = [contract(y, y, ((0,), (0,)), HIGH) for y in values]
    factors = inverse_factors(grams)
    return [
        (contract(y, m, ((1,), (1,)), HIGH) * math.sqrt(units)).astype(jnp.bfloat16)
        for y, m in zip(values, factors)
    ]


def power_kernel(splits, rows, side, *refs):
    parts = refs[: sum(splits)]
    delta_ref, keep_ref, send_ref, value, held, sem = refs[sum(splits) :]
    experts, units, _ = delta_ref.shape
    half = units // 2
    copy = pltpu.make_async_copy(delta_ref, held, sem)
    copy.start()
    at = 0
    for count, row in zip(splits, rows):
        total = parts[at][...]
        for part in parts[at + 1 : at + count]:
            total = total + part[...]
        value[:, row : row + total.shape[1]] = total
        at = at + count
    start = ranges([value[e] for e in range(experts)], units)
    copy.wait()
    own = pl.multiple_of(side[0] * half, half)
    other = pl.multiple_of((1 - side[0]) * half, half)
    for e in range(experts):
        back = contract(start[e], held[e], ((0,), (0,))).astype(jnp.bfloat16)
        keep_ref[e] = contract(held[e, pl.ds(own, half)], back, ((1,), (1,)))
        send_ref[e] = contract(held[e, pl.ds(other, half)], back, ((1,), (1,)))


def power_step(side, groups, delta):
    experts, units, _ = delta.shape
    starts, groups = zip(*groups)
    rank = groups[0][0].shape[2]
    part = jax.ShapeDtypeStruct((experts, units // 2, rank), jnp.float32)
    vmem = pl.BlockSpec(memory_space=pltpu.VMEM)
    splits = tuple(len(g) for g in groups)
    return pl.pallas_call(
        functools.partial(power_kernel, splits, starts),
        in_specs=[SMEM] + [vmem] * sum(splits) + [HBM],
        out_specs=[vmem] * 2,
        out_shape=[part, part],
        scratch_shapes=[
            pltpu.VMEM((experts, units, rank), jnp.float32),
            pltpu.VMEM(delta.shape, jnp.bfloat16),
            pltpu.SemaphoreType.DMA,
        ],
        compiler_params=params(),
    )(side, *[term for g in groups for term in g], delta)


def project_kernel(side, *refs):
    parts, (delta_ref, basis_ref, coeff_ref, value, held, sem) = refs[:-6], refs[-6:]
    experts, half, _ = parts[0].shape
    units = 2 * half
    copy = pltpu.make_async_copy(delta_ref, held, sem)
    copy.start()
    count = len(parts) // 2
    for place, group in ((side[0], parts[:count]), (1 - side[0], parts[count:])):
        total = group[0][...].astype(jnp.float32)
        for part in group[1:]:
            total = total + part[...].astype(jnp.float32)
        value[:, pl.ds(pl.multiple_of(place * half, half), half)] = total
    basis = ranges([value[e] for e in range(experts)], units)
    copy.wait()
    for e in range(experts):
        basis_ref[e] = basis[e]
        coeff = contract(basis[e], held[e], ((0,), (0,)))
        coeff_ref[e] = (coeff * (1.0 / math.sqrt(units))).astype(jnp.bfloat16)


def project(side, mine, others, delta):
    experts, units, _ = delta.shape
    rank = mine[0].shape[2]
    vmem = pl.BlockSpec(memory_space=pltpu.VMEM)
    return pl.pallas_call(
        project_kernel,
        in_specs=[SMEM] + [vmem] * (len(mine) + len(others)) + [HBM],
        out_specs=[vmem] * 2,
        out_shape=[
            jax.ShapeDtypeStruct((experts, units, rank), jnp.bfloat16),
            jax.ShapeDtypeStruct((experts, rank, delta.shape[2]), jnp.bfloat16),
        ],
        scratch_shapes=[
            pltpu.VMEM((experts, units, rank), jnp.float32),
            pltpu.VMEM(delta.shape, jnp.bfloat16),
            pltpu.SemaphoreType.DMA,
        ],
        compiler_params=params(),
    )(side, *mine, *others, delta)


def swap(value, bit, size):
    return lax.ppermute(value, "col", [(i, i ^ bit) for i in range(size)])


def sum_columns(value, size):
    bit = 1
    while 2 * bit < size:
        value = value + swap(value, bit, size)
        bit *= 2
    return value, swap(value, bit, size)


def sum_halves(keep, send, size):
    total = (keep + swap(send, 1, size)).astype(jnp.bfloat16)
    bit = 2
    while 2 * bit < size:
        total = (total.astype(jnp.float32) + swap(total, bit, size).astype(jnp.float32)).astype(
            jnp.bfloat16
        )
        bit *= 2
    far = swap(total, bit, size)
    return (total, far), (swap(total, 1, size), swap(far, 1, size))


def merge_folded(weights, fisher, member_mask, sketch, col_size):
    inwards, across, outwards = [(0, 1), (3, 2)], [(1, 2), (2, 1)], [(1, 0), (2, 3)]
    experts, units, cols = weights.shape
    clusters = member_mask.shape[1]
    place = lax.axis_index("exp")
    inner = ((place == 1) | (place == 2)).astype(jnp.int32)
    mine = lax.dynamic_slice_in_dim(member_mask, place * experts, experts)
    partner = lax.dynamic_slice_in_dim(member_mask, (place ^ 1) * experts, experts)
    mask = jnp.concatenate([mine, partner], axis=0)
    labels = jnp.argmax(mine, axis=1).astype(jnp.int32)
    meta = jnp.concatenate([labels, inner[None]])
    near = [fisher.astype(jnp.float32)]
    for hop in (1, 2, 3):
        pairs = [(i, i ^ hop) for i in range(4)]
        near.append(lax.ppermute(fisher, "exp", pairs).astype(jnp.float32))
    denom = jnp.zeros((units, clusters), jnp.float32)
    for hop, value in enumerate(near):
        rows = lax.dynamic_slice_in_dim(member_mask, (place ^ hop) * experts, experts)
        denom = denom + jnp.sum(value[:, :, None] * rows[:, None, :], axis=0)
    fcols = jnp.concatenate(near[:2], axis=0).T

    chunks = [(0, 1), (0, 2), (0, 3), (3, 3), (3, 3), (1, 3), (1, 3), (2, 3), (2, 2), (2, 1)]
    groups = [(0, 1, 2), (3, 4), (5, 6), (7,), (8, 9)]
    lead, lag = 3, 3
    spans, used = [], [0] * 4
    for q, size in chunks:
        spans.append((q * (units // 4) + used[q], size * UNIT))
        used[q] += size * UNIT
    count = len(chunks)
    their_labels = jnp.argmax(partner, axis=1).astype(jnp.int32)
    arrived, sums, others, base, moved, firsts = {}, {}, {}, {}, {}, {}
    held, after, terms = (), (), []
    for c in range(lead):
        block = weights[:, spans[c][0] : sum(spans[c])]
        arrived[c] = lax.ppermute(block, "exp", inwards)
    for step in range(count + lag):
        c = step
        if c < count:
            ahead = spans[c + lead] if c + lead < count else None
            sums[c], *copied = cluster_sums(
                mask, weights, arrived[c], fcols, *spans[c], ahead, after
            )
            others[c] = lax.ppermute(sums[c], "exp", across)
            if copied:
                arrived[c + lead] = lax.ppermute(copied[0], "exp", inwards)
            after = (sums[c],)
        c = step - 1
        if 0 <= c < count:
            whole = chunks[c][0] in (0, 3)
            result = make_base(
                sums[c], others[c], denom, spans[c][0], None if whole else their_labels, after
            )
            base[c], leaving = (result, result) if whole else result
            moved[c] = lax.ppermute(leaving, "exp", outwards)
            after = (base[c],)
        c = step - lag
        if 0 <= c < count:
            if c == count - 2:
                after = after + (moved[count - 1],)
            *held, firsts[c] = residual_chunk(
                meta, weights, base[c], moved[c], sketch, spans[c][0], held, after
            )
            after = (firsts[c],)
            for group in groups:
                if c == group[-1]:
                    joined = jnp.concatenate([firsts[g] for g in group], axis=1)
                    terms.append((spans[group[0]][0], sum_columns(joined, col_size)))
    delta, bases = held
    base = own_quarter(place[None], bases)
    return base, delta, terms


def merge_spread(weights, fisher, member_mask, sketch, col_size):
    moved = lax.all_to_all(weights, "exp", split_axis=1, concat_axis=0, tiled=True)
    f_rows = lax.all_to_all(fisher, "exp", split_axis=1, concat_axis=0, tiled=True)
    f_wide = f_rows.astype(jnp.float32)
    weighted = f_wide[:, :, None] * moved.astype(jnp.float32)
    numer = jnp.einsum("ek,erc->krc", member_mask, weighted, precision=HIGH)
    denom = jnp.einsum("ek,er->kr", member_mask, f_wide, precision=HIGH)
    base = (numer / denom[:, :, None]).astype(jnp.bfloat16)
    chosen = jnp.take(base, jnp.argmax(member_mask, axis=1), axis=0)
    residual = (moved.astype(jnp.float32) - chosen.astype(jnp.float32)).astype(jnp.bfloat16)
    delta = lax.all_to_all(residual, "exp", split_axis=0, concat_axis=1, tiled=True)
    first = jnp.einsum("nrc,nck->nrk", delta, sketch, preferred_element_type=jnp.float32)
    return base, delta, [(0, sum_columns(first, col_size))]


def body(exp_size, col_size, weights, fisher, members, sketch):
    member_mask = members.astype(jnp.float32)
    folded = exp_size == 4 and weights.shape[1] == 24 * UNIT
    merge = merge_folded if folded else merge_spread
    base, delta, first = merge(weights, fisher, member_mask, sketch, col_size)
    side = lax.rem(lax.axis_index("col"), 2)[None]
    mine, others = sum_halves(*power_step(side, first, delta), col_size)
    basis, coeff = project(side, mine, others, delta)
    return base, basis, coeff


def solution(mesh):
    in_specs = (
        P(("grp", "exp"), None, "col"),
        P(("grp", "exp"), None),
        P("grp", None),
        P(("grp", "exp"), "col", None),
    )
    out_specs = (
        P("grp", "exp", "col"),
        P(("grp", "exp"), None, None),
        P(("grp", "exp"), None, "col"),
    )
    run = functools.partial(body, mesh.shape["exp"], mesh.shape["col"])
    return jax.shard_map(run, mesh=mesh, in_specs=in_specs, out_specs=out_specs, check_vma=False)
```

```python
import functools
import math

import jax
import jax.numpy as jnp
from jax import lax
from jax.experimental import pallas as pl
from jax.experimental.pallas import tpu as pltpu
from jax.sharding import PartitionSpec as P

HIGH = lax.Precision.HIGHEST
UNIT = 32
VMEM_LIMIT = 20 * 1024 * 1024
SMEM = pl.BlockSpec(memory_space=pltpu.SMEM)


def params():
    return pltpu.CompilerParams(vmem_limit_bytes=VMEM_LIMIT)


COST = pl.CostEstimate(flops=10**10, transcendentals=0, bytes_accessed=1)
ANY = pl.BlockSpec(memory_space=pl.ANY)
HBM = pl.BlockSpec(memory_space=pltpu.HBM)


def in_hbm(array):
    return pltpu.with_memory_space_constraint(array, pltpu.HBM)


def sums_kernel(ahead, inner, mask, w_ref, a_ref, f_ref, *refs):
    experts, rows, cols = w_ref.shape
    out_ref = refs[-2] if ahead else refs[-1]
    if ahead:

        @pl.when(inner[0] == 0)
        def _():
            refs[-1][...] = refs[0][...]

    @pl.when(inner[0] == 1)
    def _():
        clusters = out_ref.shape[0]
        strip, width = 16, 512
        for r in range(0, rows, strip):
            for c in range(0, cols, width):
                totals = [jnp.zeros((strip, width), jnp.float32) for _ in range(clusters)]
                for e in range(2 * experts):
                    source = w_ref if e < experts else a_ref
                    block = source[e % experts, r : r + strip, c : c + width].astype(jnp.float32)
                    block = block * f_ref[r : r + strip, e : e + 1]
                    for k in range(clusters):
                        totals[k] = totals[k] + block * mask[e, k]
                for k in range(clusters):
                    out_ref[k, r : r + strip, c : c + width] = totals[k].astype(jnp.bfloat16)


def cluster_sums(inner, mask, weights, arrived, fcols, start, rows, ahead, after):
    experts, _, cols = weights.shape
    clusters = mask.shape[1]
    first = start // UNIT
    steps = rows // UNIT
    out_specs = [pl.BlockSpec((clusters, UNIT, cols), lambda i, on: (0, i * on[0], 0))]
    out_shape = [jax.ShapeDtypeStruct((clusters, rows, cols), jnp.bfloat16)]
    extra, extra_specs = list(after), [ANY] * len(after)
    if ahead is not None:
        begin, length = ahead
        split = length % (16 * steps) == 0 and begin % (length // steps) == 0
        part = length // steps if split else length
        shape = (experts, part, cols)
        if part != length:
            at = begin // part
            extra_specs.insert(0, pl.BlockSpec(shape, lambda i, on: (0, at + i * (1 - on[0]), 0)))
            out_specs.append(pl.BlockSpec(shape, lambda i, on: (0, i * (1 - on[0]), 0)))
        else:
            place = (pl.Element(experts), pl.Element(length), pl.Element(cols))
            extra_specs.insert(0, pl.BlockSpec(place, lambda i, on: (0, begin, 0)))
            out_specs.append(pl.BlockSpec(shape, lambda i, on: (0, 0, 0)))
        out_shape.append(jax.ShapeDtypeStruct((experts, length, cols), jnp.bfloat16))
        extra.insert(0, in_hbm(weights))
    return pl.pallas_call(
        functools.partial(sums_kernel, ahead is not None),
        grid_spec=pltpu.PrefetchScalarGridSpec(
            num_scalar_prefetch=1,
            grid=(steps,),
            in_specs=[
                SMEM,
                pl.BlockSpec((experts, UNIT, cols), lambda i, on: (0, first + i * on[0], 0)),
                pl.BlockSpec((experts, UNIT, cols), lambda i, on: (0, i * on[0], 0)),
                pl.BlockSpec((UNIT, fcols.shape[1]), lambda i, on: (first + i * on[0], 0)),
            ]
            + extra_specs,
            out_specs=out_specs,
        ),
        out_shape=out_shape,
        cost_estimate=COST,
        compiler_params=params(),
    )(inner, mask, in_hbm(weights), arrived, fcols, *extra)


def base_kernel(inner, labels, p_ref, q_ref, d_ref, *refs):
    clusters, rows, cols = p_ref.shape
    out_ref, chosen_ref = refs[-2:] if labels is not None else (refs[-1], None)

    @pl.when(inner[0] == 1)
    def _():
        scale = 1.0 / d_ref[...]
        for k in range(clusters):
            total = p_ref[k].astype(jnp.float32) + q_ref[k].astype(jnp.float32)
            out_ref[k] = (total * scale[:, k : k + 1]).astype(jnp.bfloat16)
        if chosen_ref is not None:
            for e in range(chosen_ref.shape[0]):
                chosen_ref[e] = out_ref[labels[e]]


def whole_base_kernel(inner, *refs):
    base_kernel(inner, None, *refs)


def make_base(inner, mine, other, denom, start, labels, after):
    clusters, rows, cols = mine.shape
    first = start // UNIT
    block = lambda lead: pl.BlockSpec((lead, UNIT, cols), lambda i, on: (0, i * on[0], 0))
    in_specs = [
        block(clusters),
        block(clusters),
        pl.BlockSpec((UNIT, clusters), lambda i, on: (first + i * on[0], 0)),
    ]
    shape = jax.ShapeDtypeStruct(mine.shape, jnp.bfloat16)
    kernel, operands, outs, shapes = whole_base_kernel, (), block(clusters), shape
    if labels is not None:
        kernel, operands = base_kernel, (labels,)
        in_specs = [SMEM] + in_specs
        experts = labels.shape[0]
        outs = [block(clusters), block(experts)]
        shapes = [shape, jax.ShapeDtypeStruct((experts, rows, cols), jnp.bfloat16)]
    return pl.pallas_call(
        kernel,
        grid_spec=pltpu.PrefetchScalarGridSpec(
            num_scalar_prefetch=1,
            grid=(rows // UNIT,),
            in_specs=in_specs + [ANY] * len(after),
            out_specs=outs,
        ),
        out_shape=shapes,
        cost_estimate=COST,
        compiler_params=params(),
    )(inner, *operands, mine, other, denom, *after)


def residual_kernel(meta, w_ref, b_ref, r_ref, s_ref, *refs):
    delta_ref, base_ref, first_ref = refs[-3:]
    experts = w_ref.shape[0]
    by_expert = r_ref.shape[0] == experts
    inner = meta[experts] == 1
    labels = [meta[e] for e in range(experts)]
    base_ref[...] = b_ref[...] if by_expert else r_ref[...]

    def subtract(source, indices):
        for e in range(experts):
            chosen = source[indices[e]].astype(jnp.float32)
            delta_ref[e] = (w_ref[e].astype(jnp.float32) - chosen).astype(jnp.bfloat16)

    @pl.when(inner)
    def _():
        subtract(b_ref, labels)

    @pl.when(jnp.logical_not(inner))
    def _():
        subtract(r_ref, range(experts) if by_expert else labels)

    for e in range(experts):
        first_ref[e] = jnp.dot(delta_ref[e], s_ref[e], preferred_element_type=jnp.float32)


def residual_chunk(meta, weights, base, arrived, sketch, quarter, start, held, after):
    experts, units, cols = weights.shape
    clusters, rows, _ = base.shape
    rank = sketch.shape[2]
    first = start // UNIT
    quarter_blocks = units // 4 // UNIT
    local = first - quarter * quarter_blocks
    own = lambda meta: meta[experts + 1] == quarter

    def keep(i, meta):
        return (0, jnp.where(own(meta), local + i, quarter_blocks), 0)

    chunk = lambda lead: pl.BlockSpec((lead, UNIT, cols), lambda i, meta: (0, i, 0))
    placed = pl.BlockSpec((experts, UNIT, cols), lambda i, meta: (0, first + i, 0))
    return pl.pallas_call(
        residual_kernel,
        grid_spec=pltpu.PrefetchScalarGridSpec(
            num_scalar_prefetch=1,
            grid=(rows // UNIT,),
            in_specs=[
                placed,
                chunk(clusters),
                chunk(arrived.shape[0]),
                pl.BlockSpec(sketch.shape, lambda i, meta: (0, 0, 0)),
            ]
            + [HBM] * len(held)
            + [ANY] * len(after),
            out_specs=[
                placed,
                pl.BlockSpec((clusters, UNIT, cols), keep),
                pl.BlockSpec((experts, UNIT, rank), lambda i, meta: (0, i, 0)),
            ],
        ),
        out_shape=[
            pltpu.HBM((experts, units, cols), jnp.bfloat16),
            pltpu.HBM((clusters, units // 4 + UNIT, cols), jnp.bfloat16),
            jax.ShapeDtypeStruct((experts, rows, rank), jnp.float32),
        ],
        cost_estimate=COST,
        input_output_aliases={5 + i: i for i in range(len(held))},
        compiler_params=params(),
    )(meta, in_hbm(weights), base, arrived, sketch, *held, *after)


def copy_kernel(in_ref, out_ref):
    out_ref[...] = in_ref[...]


def leading_rows(array, rows):
    lead, _, cols = array.shape
    block = pl.BlockSpec((lead, rows, cols // 2), lambda i: (0, 0, i))
    return pl.pallas_call(
        copy_kernel,
        grid=(2,),
        in_specs=[block],
        out_specs=block,
        out_shape=jax.ShapeDtypeStruct((lead, rows, cols), array.dtype),
        compiler_params=params(),
    )(array)


GROUP = 8


def inverse_factors(grams):
    size = grams[0].shape[0]
    lane = lax.broadcasted_iota(jnp.int32, (GROUP, size), 1)
    sub = lax.broadcasted_iota(jnp.int32, (GROUP, size), 0)
    groups = range(size // GROUP)
    tables = [[g[i * GROUP : (i + 1) * GROUP] for i in groups] for g in grams]
    for at in groups:
        first = at * GROUP
        block = (lane >= first) & (lane < first + GROUP)
        unit = jnp.where(lane - first == sub, 1.0, 0.0)
        for table in tables:
            own = table[at]
            cols = [
                jnp.broadcast_to(own[:, first + t : first + t + 1], (GROUP, size))
                for t in range(GROUP)
            ]
            rows = jnp.where(block, unit, own)
            diag = cols[0]
            for t in range(GROUP - 1):
                factor = jnp.where(sub > t, cols[t] * (1.0 / cols[t][t : t + 1]), 0.0)
                for s in range(t + 1, GROUP):
                    cols[s] = cols[s] - factor * cols[s][t : t + 1]
                rows = rows - factor * rows[t : t + 1]
                diag = jnp.where(sub > t, cols[t + 1], diag)
            inverse = 1.0 / diag
            table[at] = rows * lax.rsqrt(diag)
            solved = rows * inverse
            for t in range(GROUP - 1, 0, -1):
                upper = jnp.where(sub < t, cols[t] * inverse, 0.0)
                solved = solved - upper * solved[t : t + 1]
            for i in range(at + 1, size // GROUP):
                value = table[i]
                rest = jnp.where(block, 0.0, value)
                for t in range(GROUP):
                    col = jnp.broadcast_to(value[:, first + t : first + t + 1], (GROUP, size))
                    rest = rest - col * solved[t : t + 1]
                table[i] = rest
    out = []
    for table in tables:
        parts = [jnp.where(lane <= sub + i * GROUP, table[i], 0.0) for i in groups]
        out.append(jnp.concatenate(parts, axis=0))
    return out


def contract(left, right, dims, precision=None):
    return lax.dot_general(
        left, right, (dims, ((), ())), precision=precision, preferred_element_type=jnp.float32
    )


def ranges(values, units):
    grams = [contract(y, y, ((0,), (0,)), HIGH) for y in values]
    factors = inverse_factors(grams)
    return [
        (contract(y, m, ((1,), (1,)), HIGH) * math.sqrt(units)).astype(jnp.bfloat16)
        for y, m in zip(values, factors)
    ]


def power_kernel(splits, pieces, side, *refs):
    parts = refs[: sum(splits)]
    delta_ref = refs[sum(splits)]
    keep_ref, send_ref, value, held, sem = refs[-5:]
    experts, units, _ = delta_ref.shape
    half = units // 2
    copy = pltpu.make_async_copy(delta_ref, held, sem)
    copy.start()
    at = 0
    for count, places in zip(splits, pieces):
        total = parts[at][...]
        for part in parts[at + 1 : at + count]:
            total = total + part[...]
        row = 0
        for start, rows in places:
            value[:, start : start + rows] = total[:, row : row + rows]
            row += rows
        at = at + count
    start = ranges([value[e] for e in range(experts)], units)
    copy.wait()
    own = pl.multiple_of(side[0] * half, half)
    other = pl.multiple_of((1 - side[0]) * half, half)
    for e in range(experts):
        back = contract(start[e], held[e], ((0,), (0,))).astype(jnp.bfloat16)
        keep_ref[e] = contract(held[e, pl.ds(own, half)], back, ((1,), (1,)))
        send_ref[e] = contract(held[e, pl.ds(other, half)], back, ((1,), (1,)))


def power_step(side, groups, delta):
    experts, units, _ = delta.shape
    pieces, groups = zip(*groups)
    rank = groups[0][0].shape[2]
    part = jax.ShapeDtypeStruct((experts, units // 2, rank), jnp.float32)
    vmem = pl.BlockSpec(memory_space=pltpu.VMEM)
    splits = tuple(len(g) for g in groups)
    return pl.pallas_call(
        functools.partial(power_kernel, splits, pieces),
        in_specs=[SMEM] + [vmem] * sum(splits) + [HBM],
        out_specs=[vmem] * 2,
        out_shape=[part, part],
        scratch_shapes=[
            pltpu.VMEM((experts, units, rank), jnp.float32),
            pltpu.VMEM(delta.shape, jnp.bfloat16),
            pltpu.SemaphoreType.DMA,
        ],
        compiler_params=params(),
    )(side, *[term for g in groups for term in g], delta)


def project_kernel(side, *refs):
    parts, (delta_ref, basis_ref, coeff_ref, value, held, sem) = refs[:-6], refs[-6:]
    experts, half, _ = parts[0].shape
    units = 2 * half
    copy = pltpu.make_async_copy(delta_ref, held, sem)
    copy.start()
    count = len(parts) // 2
    for place, group in ((side[0], parts[:count]), (1 - side[0], parts[count:])):
        total = group[0][...].astype(jnp.float32)
        for part in group[1:]:
            total = total + part[...].astype(jnp.float32)
        value[:, pl.ds(pl.multiple_of(place * half, half), half)] = total
    basis = ranges([value[e] for e in range(experts)], units)
    copy.wait()
    for e in range(experts):
        basis_ref[e] = basis[e]
        coeff = contract(basis[e], held[e], ((0,), (0,)))
        coeff_ref[e] = (coeff * (1.0 / math.sqrt(units))).astype(jnp.bfloat16)


def project(side, mine, others, delta):
    experts, units, _ = delta.shape
    rank = mine[0].shape[2]
    vmem = pl.BlockSpec(memory_space=pltpu.VMEM)
    return pl.pallas_call(
        project_kernel,
        in_specs=[SMEM] + [vmem] * (len(mine) + len(others)) + [HBM],
        out_specs=[vmem] * 2,
        out_shape=[
            jax.ShapeDtypeStruct((experts, units, rank), jnp.bfloat16),
            jax.ShapeDtypeStruct((experts, rank, delta.shape[2]), jnp.bfloat16),
        ],
        scratch_shapes=[
            pltpu.VMEM((experts, units, rank), jnp.float32),
            pltpu.VMEM(delta.shape, jnp.bfloat16),
            pltpu.SemaphoreType.DMA,
        ],
        compiler_params=params(),
    )(side, *mine, *others, delta)


def swap(value, bit, size):
    return lax.ppermute(value, "col", [(i, i ^ bit) for i in range(size)])


def sum_columns(value, size):
    bit = 1
    while 2 * bit < size:
        value = value + swap(value, bit, size)
        bit *= 2
    return value, swap(value, bit, size)


def sum_halves(keep, send, size):
    total = (keep + swap(send, 1, size)).astype(jnp.bfloat16)
    bit = 2
    while 2 * bit < size:
        total = (total.astype(jnp.float32) + swap(total, bit, size).astype(jnp.float32)).astype(
            jnp.bfloat16
        )
        bit *= 2
    far = swap(total, bit, size)
    return (total, far), (swap(total, 1, size), swap(far, 1, size))


def merge_folded(weights, fisher, member_mask, sketch, col_size):
    inwards, across, outwards = [(0, 1), (3, 2)], [(1, 2), (2, 1)], [(1, 0), (2, 3)]
    experts, units, cols = weights.shape
    clusters = member_mask.shape[1]
    place = lax.axis_index("exp")
    inner = ((place == 1) | (place == 2)).astype(jnp.int32)[None]
    mine = lax.dynamic_slice_in_dim(member_mask, place * experts, experts)
    partner = lax.dynamic_slice_in_dim(member_mask, (place ^ 1) * experts, experts)
    mask = jnp.concatenate([mine, partner], axis=0)
    meta = jnp.concatenate([jnp.argmax(mine, axis=1).astype(jnp.int32), inner, place[None]])
    opening = weights[:, : UNIT]
    fisher, opening = lax.optimization_barrier((fisher, opening))
    near = [fisher.astype(jnp.float32)]
    for hop in (1, 2, 3):
        pairs = [(i, i ^ hop) for i in range(4)]
        near.append(lax.ppermute(fisher, "exp", pairs).astype(jnp.float32))
    denom = jnp.zeros((units, clusters), jnp.float32)
    for hop, value in enumerate(near):
        rows = lax.dynamic_slice_in_dim(member_mask, (place ^ hop) * experts, experts)
        denom = denom + jnp.sum(value[:, :, None] * rows[:, None, :], axis=0)
    fcols = jnp.concatenate(near[:2], axis=0).T

    chunks = [(0, 1), (0, 2), (0, 3), (3, 3), (3, 3), (1, 3), (1, 3), (2, 3), (2, 2), (2, 1)]
    groups = [(0, 1, 2, 3, 4), (5, 6, 7, 8), (9,)]
    lead, lag = 2, 2
    spans, used = [], [0] * 4
    for q, size in chunks:
        spans.append((q * (units // 4) + used[q], size * UNIT))
        used[q] += size * UNIT
    count = len(chunks)
    their_labels = jnp.argmax(partner, axis=1).astype(jnp.int32)
    arrived, sums, others, base, moved, firsts = {}, {}, {}, {}, {}, {}
    held, after, terms, ready = (), (), [], {}
    for c in range(lead):
        block = weights[:, spans[c][0] : sum(spans[c])] if c else opening
        arrived[c] = lax.ppermute(block, "exp", inwards)
    order = []
    for step in range(count):
        order += [("sums", step), ("base", step - 1), ("residual", step - lag)]
    order += [("base", count - 1)] + [("residual", c) for c in range(count - lag, count)]
    for kind, c in order:
        if c < 0:
            continue
        if kind == "sums":
            ahead = spans[c + lead] if c + lead < count else None
            sums[c], *copied = cluster_sums(
                inner, mask, weights, arrived[c], fcols, *spans[c], ahead, after
            )
            others[c] = lax.ppermute(sums[c], "exp", across)
            if copied:
                arrived[c + lead] = lax.ppermute(copied[0], "exp", inwards)
            after = (sums[c],)
        elif kind == "base":
            whole = chunks[c][0] in (0, 3)
            labels = None if whole else their_labels
            result = make_base(inner, sums[c], others[c], denom, spans[c][0], labels, after)
            base[c], leaving = (result, result) if whole else result
            moved[c] = lax.ppermute(leaving, "exp", outwards)
            after = (base[c],)
        else:
            *held, firsts[c] = residual_chunk(
                meta,
                weights,
                base[c],
                moved[c],
                sketch,
                chunks[c][0],
                spans[c][0],
                held,
                after + ready.pop(c, ()),
            )
            after = (firsts[c],)
            for group in groups:
                if c == group[-1]:
                    joined = jnp.concatenate([firsts[g] for g in group], axis=1)
                    total = sum_columns(joined, col_size)
                    terms.append((tuple(spans[g] for g in group), total))
                    ready[c + 2] = total[1:]
    delta, bases = held
    base = leading_rows(bases, units // 4)
    return base, delta, terms


def merge_spread(weights, fisher, member_mask, sketch, col_size):
    moved = lax.all_to_all(weights, "exp", split_axis=1, concat_axis=0, tiled=True)
    f_rows = lax.all_to_all(fisher, "exp", split_axis=1, concat_axis=0, tiled=True)
    f_wide = f_rows.astype(jnp.float32)
    weighted = f_wide[:, :, None] * moved.astype(jnp.float32)
    numer = jnp.einsum("ek,erc->krc", member_mask, weighted, precision=HIGH)
    denom = jnp.einsum("ek,er->kr", member_mask, f_wide, precision=HIGH)
    base = (numer / denom[:, :, None]).astype(jnp.bfloat16)
    chosen = jnp.take(base, jnp.argmax(member_mask, axis=1), axis=0)
    residual = (moved.astype(jnp.float32) - chosen.astype(jnp.float32)).astype(jnp.bfloat16)
    delta = lax.all_to_all(residual, "exp", split_axis=0, concat_axis=1, tiled=True)
    first = jnp.einsum("nrc,nck->nrk", delta, sketch, preferred_element_type=jnp.float32)
    return base, delta, [(((0, first.shape[1]),), sum_columns(first, col_size))]


def body(exp_size, col_size, weights, fisher, members, sketch):
    member_mask = members.astype(jnp.float32)
    folded = exp_size == 4 and weights.shape[1] == 24 * UNIT
    merge = merge_folded if folded else merge_spread
    base, delta, first = merge(weights, fisher, member_mask, sketch, col_size)
    side = lax.rem(lax.axis_index("col"), 2)[None]
    mine, others = sum_halves(*power_step(side, first, delta), col_size)
    basis, coeff = project(side, mine, others, delta)
    return base, basis, coeff


def solution(mesh):
    in_specs = (
        P(("grp", "exp"), None, "col"),
        P(("grp", "exp"), None),
        P("grp", None),
        P(("grp", "exp"), "col", None),
    )
    out_specs = (
        P("grp", "exp", "col"),
        P(("grp", "exp"), None, None),
        P(("grp", "exp"), None, "col"),
    )
    run = functools.partial(body, mesh.shape["exp"], mesh.shape["col"])
    return jax.shard_map(run, mesh=mesh, in_specs=in_specs, out_specs=out_specs, check_vma=False)
```

```python
import functools
import math

import jax
import jax.numpy as jnp
from jax import lax
from jax.experimental import pallas as pl
from jax.experimental.pallas import tpu as pltpu
from jax.sharding import PartitionSpec as P

HIGH = lax.Precision.HIGHEST
UNIT = 32
VMEM_LIMIT = 20 * 1024 * 1024
SMEM = pl.BlockSpec(memory_space=pltpu.SMEM)


def params():
    return pltpu.CompilerParams(vmem_limit_bytes=VMEM_LIMIT)


COST = pl.CostEstimate(flops=10**10, transcendentals=0, bytes_accessed=1)
ANY = pl.BlockSpec(memory_space=pl.ANY)
HBM = pl.BlockSpec(memory_space=pltpu.HBM)


def in_hbm(array):
    return pltpu.with_memory_space_constraint(array, pltpu.HBM)


def sums_kernel(ahead, inner, mask, w_ref, a_ref, f_ref, *refs):
    experts, rows, cols = w_ref.shape
    out_ref = refs[-2] if ahead else refs[-1]
    if ahead:

        @pl.when(inner[0] == 0)
        def _():
            refs[-1][...] = refs[0][...]

    @pl.when(inner[0] == 1)
    def _():
        clusters = out_ref.shape[0]
        strip, width = 16, 512
        across = cols // width

        def one(n, carry):
            r = pl.multiple_of((n // across) * strip, strip)
            c = pl.multiple_of((n % across) * width, width)
            at = (pl.ds(r, strip), pl.ds(c, width))
            totals = [jnp.zeros((strip, width), jnp.float32) for _ in range(clusters)]
            for e in range(2 * experts):
                source = w_ref if e < experts else a_ref
                block = source[e % experts, at[0], at[1]].astype(jnp.float32)
                block = block * f_ref[pl.ds(r, strip), e : e + 1]
                for k in range(clusters):
                    totals[k] = totals[k] + block * mask[e, k]
            for k in range(clusters):
                out_ref[k, at[0], at[1]] = totals[k].astype(jnp.bfloat16)
            return carry

        lax.fori_loop(0, (rows // strip) * across, one, 0)


def cluster_sums(inner, mask, weights, arrived, fcols, start, rows, ahead, after):
    experts, _, cols = weights.shape
    clusters = mask.shape[1]
    first = start // UNIT
    steps = rows // UNIT
    out_specs = [pl.BlockSpec((clusters, UNIT, cols), lambda i, on: (0, i * on[0], 0))]
    out_shape = [jax.ShapeDtypeStruct((clusters, rows, cols), jnp.bfloat16)]
    extra, extra_specs = list(after), [ANY] * len(after)
    if ahead is not None:
        begin, length = ahead
        split = length % (16 * steps) == 0 and begin % (length // steps) == 0
        part = length // steps if split else length
        shape = (experts, part, cols)
        if part != length:
            at = begin // part
            extra_specs.insert(0, pl.BlockSpec(shape, lambda i, on: (0, at + i * (1 - on[0]), 0)))
            out_specs.append(pl.BlockSpec(shape, lambda i, on: (0, i * (1 - on[0]), 0)))
        else:
            place = (pl.Element(experts), pl.Element(length), pl.Element(cols))
            extra_specs.insert(0, pl.BlockSpec(place, lambda i, on: (0, begin, 0)))
            out_specs.append(pl.BlockSpec(shape, lambda i, on: (0, 0, 0)))
        out_shape.append(jax.ShapeDtypeStruct((experts, length, cols), jnp.bfloat16))
        extra.insert(0, in_hbm(weights))
    return pl.pallas_call(
        functools.partial(sums_kernel, ahead is not None),
        grid_spec=pltpu.PrefetchScalarGridSpec(
            num_scalar_prefetch=1,
            grid=(steps,),
            in_specs=[
                SMEM,
                pl.BlockSpec((experts, UNIT, cols), lambda i, on: (0, first + i * on[0], 0)),
                pl.BlockSpec((experts, UNIT, cols), lambda i, on: (0, i * on[0], 0)),
                pl.BlockSpec((UNIT, fcols.shape[1]), lambda i, on: (first + i * on[0], 0)),
            ]
            + extra_specs,
            out_specs=out_specs,
        ),
        out_shape=out_shape,
        cost_estimate=COST,
        compiler_params=params(),
    )(inner, mask, in_hbm(weights), arrived, fcols, *extra)


def base_kernel(inner, labels, p_ref, q_ref, d_ref, *refs):
    clusters, rows, cols = p_ref.shape
    out_ref, chosen_ref = refs[-2:] if labels is not None else (refs[-1], None)

    @pl.when(inner[0] == 1)
    def _():
        scale = 1.0 / d_ref[...]
        for k in range(clusters):
            total = p_ref[k].astype(jnp.float32) + q_ref[k].astype(jnp.float32)
            out_ref[k] = (total * scale[:, k : k + 1]).astype(jnp.bfloat16)
        if chosen_ref is not None:
            for e in range(chosen_ref.shape[0]):
                chosen_ref[e] = out_ref[labels[e]]


def whole_base_kernel(inner, *refs):
    base_kernel(inner, None, *refs)


def make_base(inner, mine, other, denom, start, labels, after):
    clusters, rows, cols = mine.shape
    first = start // UNIT
    block = lambda lead: pl.BlockSpec((lead, UNIT, cols), lambda i, on: (0, i * on[0], 0))
    in_specs = [
        block(clusters),
        block(clusters),
        pl.BlockSpec((UNIT, clusters), lambda i, on: (first + i * on[0], 0)),
    ]
    shape = jax.ShapeDtypeStruct(mine.shape, jnp.bfloat16)
    kernel, operands, outs, shapes = whole_base_kernel, (), block(clusters), shape
    if labels is not None:
        kernel, operands = base_kernel, (labels,)
        in_specs = [SMEM] + in_specs
        experts = labels.shape[0]
        outs = [block(clusters), block(experts)]
        shapes = [shape, jax.ShapeDtypeStruct((experts, rows, cols), jnp.bfloat16)]
    return pl.pallas_call(
        kernel,
        grid_spec=pltpu.PrefetchScalarGridSpec(
            num_scalar_prefetch=1,
            grid=(rows // UNIT,),
            in_specs=in_specs + [ANY] * len(after),
            out_specs=outs,
        ),
        out_shape=shapes,
        cost_estimate=COST,
        compiler_params=params(),
    )(inner, *operands, mine, other, denom, *after)


def residual_kernel(meta, w_ref, b_ref, r_ref, s_ref, *refs):
    delta_ref, base_ref, first_ref = refs[-3:]
    experts = w_ref.shape[0]
    by_expert = r_ref.shape[0] == experts
    inner = meta[experts] == 1
    labels = [meta[e] for e in range(experts)]
    base_ref[...] = b_ref[...] if by_expert else r_ref[...]

    def subtract(source, indices):
        for e in range(experts):
            chosen = source[indices[e]].astype(jnp.float32)
            delta_ref[e] = (w_ref[e].astype(jnp.float32) - chosen).astype(jnp.bfloat16)

    @pl.when(inner)
    def _():
        subtract(b_ref, labels)

    @pl.when(jnp.logical_not(inner))
    def _():
        subtract(r_ref, range(experts) if by_expert else labels)

    for e in range(experts):
        first_ref[e] = jnp.dot(delta_ref[e], s_ref[e], preferred_element_type=jnp.float32)


def residual_chunk(meta, weights, base, arrived, sketch, quarter, start, held, after):
    experts, units, cols = weights.shape
    clusters, rows, _ = base.shape
    rank = sketch.shape[2]
    first = start // UNIT
    quarter_blocks = units // 4 // UNIT
    local = first - quarter * quarter_blocks
    own = lambda meta: meta[experts + 1] == quarter

    def keep(i, meta):
        return (0, jnp.where(own(meta), local + i, quarter_blocks), 0)

    chunk = lambda lead: pl.BlockSpec((lead, UNIT, cols), lambda i, meta: (0, i, 0))
    placed = pl.BlockSpec((experts, UNIT, cols), lambda i, meta: (0, first + i, 0))
    return pl.pallas_call(
        residual_kernel,
        grid_spec=pltpu.PrefetchScalarGridSpec(
            num_scalar_prefetch=1,
            grid=(rows // UNIT,),
            in_specs=[
                placed,
                chunk(clusters),
                chunk(arrived.shape[0]),
                pl.BlockSpec(sketch.shape, lambda i, meta: (0, 0, 0)),
            ]
            + [HBM] * len(held)
            + [ANY] * len(after),
            out_specs=[
                placed,
                pl.BlockSpec((clusters, UNIT, cols), keep),
                pl.BlockSpec((experts, UNIT, rank), lambda i, meta: (0, i, 0)),
            ],
        ),
        out_shape=[
            pltpu.HBM((experts, units, cols), jnp.bfloat16),
            pltpu.HBM((clusters, units // 4 + UNIT, cols), jnp.bfloat16),
            jax.ShapeDtypeStruct((experts, rows, rank), jnp.float32),
        ],
        cost_estimate=COST,
        input_output_aliases={5 + i: i for i in range(len(held))},
        compiler_params=params(),
    )(meta, in_hbm(weights), base, arrived, sketch, *held, *after)


def copy_kernel(in_ref, out_ref):
    out_ref[...] = in_ref[...]


def leading_rows(array, rows):
    lead, _, cols = array.shape
    block = pl.BlockSpec((lead, rows, cols // 2), lambda i: (0, 0, i))
    return pl.pallas_call(
        copy_kernel,
        grid=(2,),
        in_specs=[block],
        out_specs=block,
        out_shape=jax.ShapeDtypeStruct((lead, rows, cols), array.dtype),
        compiler_params=params(),
    )(array)


GROUP = 8


def inverse_factors(grams):
    size = grams[0].shape[0]
    lane = lax.broadcasted_iota(jnp.int32, (GROUP, size), 1)
    sub = lax.broadcasted_iota(jnp.int32, (GROUP, size), 0)
    groups = range(size // GROUP)
    tables = [[g[i * GROUP : (i + 1) * GROUP] for i in groups] for g in grams]
    for at in groups:
        first = at * GROUP
        block = (lane >= first) & (lane < first + GROUP)
        unit = jnp.where(lane - first == sub, 1.0, 0.0)
        for table in tables:
            own = table[at]
            cols = [
                jnp.broadcast_to(own[:, first + t : first + t + 1], (GROUP, size))
                for t in range(GROUP)
            ]
            rows = jnp.where(block, unit, own)
            diag = cols[0]
            for t in range(GROUP - 1):
                factor = jnp.where(sub > t, cols[t] * (1.0 / cols[t][t : t + 1]), 0.0)
                for s in range(t + 1, GROUP):
                    cols[s] = cols[s] - factor * cols[s][t : t + 1]
                rows = rows - factor * rows[t : t + 1]
                diag = jnp.where(sub > t, cols[t + 1], diag)
            inverse = 1.0 / diag
            table[at] = rows * lax.rsqrt(diag)
            solved = rows * inverse
            for t in range(GROUP - 1, 0, -1):
                upper = jnp.where(sub < t, cols[t] * inverse, 0.0)
                solved = solved - upper * solved[t : t + 1]
            for i in range(at + 1, size // GROUP):
                value = table[i]
                rest = jnp.where(block, 0.0, value)
                for t in range(GROUP):
                    col = jnp.broadcast_to(value[:, first + t : first + t + 1], (GROUP, size))
                    rest = rest - col * solved[t : t + 1]
                table[i] = rest
    out = []
    for table in tables:
        parts = [jnp.where(lane <= sub + i * GROUP, table[i], 0.0) for i in groups]
        out.append(jnp.concatenate(parts, axis=0))
    return out


def contract(left, right, dims, precision=None):
    return lax.dot_general(
        left, right, (dims, ((), ())), precision=precision, preferred_element_type=jnp.float32
    )


def ranges(values, units):
    grams = [contract(y, y, ((0,), (0,)), HIGH) for y in values]
    factors = inverse_factors(grams)
    return [
        (contract(y, m, ((1,), (1,)), HIGH) * math.sqrt(units)).astype(jnp.bfloat16)
        for y, m in zip(values, factors)
    ]


def power_kernel(splits, pieces, side, *refs):
    parts = refs[: sum(splits)]
    delta_ref = refs[sum(splits)]
    keep_ref, send_ref, value, held, sem = refs[-5:]
    experts, units, _ = delta_ref.shape
    half = units // 2
    copy = pltpu.make_async_copy(delta_ref, held, sem)
    copy.start()
    at = 0
    for count, places in zip(splits, pieces):
        total = parts[at][...].astype(jnp.float32)
        for part in parts[at + 1 : at + count]:
            total = total + part[...].astype(jnp.float32)
        row = 0
        for start, rows in places:
            value[:, start : start + rows] = total[:, row : row + rows]
            row += rows
        at = at + count
    start = ranges([value[e] for e in range(experts)], units)
    copy.wait()
    own = pl.multiple_of(side[0] * half, half)
    other = pl.multiple_of((1 - side[0]) * half, half)
    for e in range(experts):
        back = contract(start[e], held[e], ((0,), (0,))).astype(jnp.bfloat16)
        keep_ref[e] = contract(held[e, pl.ds(own, half)], back, ((1,), (1,)))
        send_ref[e] = contract(held[e, pl.ds(other, half)], back, ((1,), (1,)))


def power_step(side, groups, delta):
    experts, units, _ = delta.shape
    pieces, groups = zip(*groups)
    rank = groups[0][0].shape[2]
    part = jax.ShapeDtypeStruct((experts, units // 2, rank), jnp.float32)
    vmem = pl.BlockSpec(memory_space=pltpu.VMEM)
    splits = tuple(len(g) for g in groups)
    return pl.pallas_call(
        functools.partial(power_kernel, splits, pieces),
        in_specs=[SMEM] + [vmem] * sum(splits) + [HBM],
        out_specs=[vmem] * 2,
        out_shape=[part, part],
        scratch_shapes=[
            pltpu.VMEM((experts, units, rank), jnp.float32),
            pltpu.VMEM(delta.shape, jnp.bfloat16),
            pltpu.SemaphoreType.DMA,
        ],
        compiler_params=params(),
    )(side, *[term for g in groups for term in g], delta)


def project_kernel(side, *refs):
    parts, (delta_ref, basis_ref, coeff_ref, value, held, sem) = refs[:-6], refs[-6:]
    experts, half, _ = parts[0].shape
    units = 2 * half
    copy = pltpu.make_async_copy(delta_ref, held, sem)
    copy.start()
    count = len(parts) // 2
    for place, group in ((side[0], parts[:count]), (1 - side[0], parts[count:])):
        total = group[0][...].astype(jnp.float32)
        for part in group[1:]:
            total = total + part[...].astype(jnp.float32)
        value[:, pl.ds(pl.multiple_of(place * half, half), half)] = total
    basis = ranges([value[e] for e in range(experts)], units)
    copy.wait()
    for e in range(experts):
        basis_ref[e] = basis[e]
        coeff = contract(basis[e], held[e], ((0,), (0,)))
        coeff_ref[e] = (coeff * (1.0 / math.sqrt(units))).astype(jnp.bfloat16)


def project(side, mine, others, delta):
    experts, units, _ = delta.shape
    rank = mine[0].shape[2]
    vmem = pl.BlockSpec(memory_space=pltpu.VMEM)
    return pl.pallas_call(
        project_kernel,
        in_specs=[SMEM] + [vmem] * (len(mine) + len(others)) + [HBM],
        out_specs=[vmem] * 2,
        out_shape=[
            jax.ShapeDtypeStruct((experts, units, rank), jnp.bfloat16),
            jax.ShapeDtypeStruct((experts, rank, delta.shape[2]), jnp.bfloat16),
        ],
        scratch_shapes=[
            pltpu.VMEM((experts, units, rank), jnp.float32),
            pltpu.VMEM(delta.shape, jnp.bfloat16),
            pltpu.SemaphoreType.DMA,
        ],
        compiler_params=params(),
    )(side, *mine, *others, delta)


def swap(value, bit, size):
    return lax.ppermute(value, "col", [(i, i ^ bit) for i in range(size)])


def sum_columns(value, size):
    bit = 1
    while 2 * bit < size:
        value = value + swap(value, bit, size)
        bit *= 2
    value = value.astype(jnp.bfloat16)
    return value, swap(value, bit, size)


def sum_halves(keep, send, size):
    total = (keep + swap(send, 1, size)).astype(jnp.bfloat16)
    bit = 2
    while 2 * bit < size:
        total = (total.astype(jnp.float32) + swap(total, bit, size).astype(jnp.float32)).astype(
            jnp.bfloat16
        )
        bit *= 2
    far = swap(total, bit, size)
    return (total, far), (swap(total, 1, size), swap(far, 1, size))


def merge_folded(weights, fisher, member_mask, sketch, col_size):
    inwards, across, outwards = [(0, 1), (3, 2)], [(1, 2), (2, 1)], [(1, 0), (2, 3)]
    experts, units, cols = weights.shape
    clusters = member_mask.shape[1]
    place = lax.axis_index("exp")
    inner = ((place == 1) | (place == 2)).astype(jnp.int32)[None]
    mine = lax.dynamic_slice_in_dim(member_mask, place * experts, experts)
    partner = lax.dynamic_slice_in_dim(member_mask, (place ^ 1) * experts, experts)
    mask = jnp.concatenate([mine, partner], axis=0)
    meta = jnp.concatenate([jnp.argmax(mine, axis=1).astype(jnp.int32), inner, place[None]])
    opening = weights[:, : UNIT]
    fisher, opening = lax.optimization_barrier((fisher, opening))
    near = [fisher.astype(jnp.float32)]
    for hop in (1, 2, 3):
        pairs = [(i, i ^ hop) for i in range(4)]
        near.append(lax.ppermute(fisher, "exp", pairs).astype(jnp.float32))
    denom = jnp.zeros((units, clusters), jnp.float32)
    for hop, value in enumerate(near):
        rows = lax.dynamic_slice_in_dim(member_mask, (place ^ hop) * experts, experts)
        denom = denom + jnp.sum(value[:, :, None] * rows[:, None, :], axis=0)
    fcols = jnp.concatenate(near[:2], axis=0).T

    chunks = [(0, 1), (0, 2), (0, 3), (3, 3), (3, 3), (1, 3), (1, 3), (2, 3), (2, 2), (2, 1)]
    groups = [(0, 1, 2, 3, 4), (5, 6, 7), (8, 9)]
    lead, lag = 2, 2
    spans, used = [], [0] * 4
    for q, size in chunks:
        spans.append((q * (units // 4) + used[q], size * UNIT))
        used[q] += size * UNIT
    count = len(chunks)
    their_labels = jnp.argmax(partner, axis=1).astype(jnp.int32)
    arrived, sums, others, base, moved, firsts = {}, {}, {}, {}, {}, {}
    held, after, terms, ready = (), (), [], {}
    for c in range(lead):
        block = weights[:, spans[c][0] : sum(spans[c])] if c else opening
        arrived[c] = lax.ppermute(block, "exp", inwards)
    order = []
    for step in range(count):
        order += [("sums", step), ("base", step - 1), ("residual", step - lag)]
    order += [("base", count - 1)] + [("residual", c) for c in range(count - lag, count)]
    for kind, c in order:
        if c < 0:
            continue
        if kind == "sums":
            ahead = spans[c + lead] if c + lead < count else None
            sums[c], *copied = cluster_sums(
                inner, mask, weights, arrived[c], fcols, *spans[c], ahead, after
            )
            others[c] = lax.ppermute(sums[c], "exp", across)
            if copied:
                arrived[c + lead] = lax.ppermute(copied[0], "exp", inwards)
            after = (sums[c],)
        elif kind == "base":
            whole = chunks[c][0] in (0, 3)
            labels = None if whole else their_labels
            result = make_base(inner, sums[c], others[c], denom, spans[c][0], labels, after)
            base[c], leaving = (result, result) if whole else result
            moved[c] = lax.ppermute(leaving, "exp", outwards)
            after = (base[c],)
        else:
            if c == count - 2:
                after = after + (moved[count - 1],)
            *held, firsts[c] = residual_chunk(
                meta,
                weights,
                base[c],
                moved[c],
                sketch,
                chunks[c][0],
                spans[c][0],
                held,
                after + ready.pop(c, ()),
            )
            after = (firsts[c],)
            for group in groups:
                if c == group[-1]:
                    joined = jnp.concatenate([firsts[g] for g in group], axis=1)
                    total = sum_columns(joined, col_size)
                    terms.append((tuple(spans[g] for g in group), total))
                    ready[c + 2] = total[1:]
    delta, bases = held
    base = leading_rows(bases, units // 4)
    return base, delta, terms


def merge_spread(weights, fisher, member_mask, sketch, col_size):
    moved = lax.all_to_all(weights, "exp", split_axis=1, concat_axis=0, tiled=True)
    f_rows = lax.all_to_all(fisher, "exp", split_axis=1, concat_axis=0, tiled=True)
    f_wide = f_rows.astype(jnp.float32)
    weighted = f_wide[:, :, None] * moved.astype(jnp.float32)
    numer = jnp.einsum("ek,erc->krc", member_mask, weighted, precision=HIGH)
    denom = jnp.einsum("ek,er->kr", member_mask, f_wide, precision=HIGH)
    base = (numer / denom[:, :, None]).astype(jnp.bfloat16)
    chosen = jnp.take(base, jnp.argmax(member_mask, axis=1), axis=0)
    residual = (moved.astype(jnp.float32) - chosen.astype(jnp.float32)).astype(jnp.bfloat16)
    delta = lax.all_to_all(residual, "exp", split_axis=0, concat_axis=1, tiled=True)
    first = jnp.einsum("nrc,nck->nrk", delta, sketch, preferred_element_type=jnp.float32)
    return base, delta, [(((0, first.shape[1]),), sum_columns(first, col_size))]


def body(exp_size, col_size, weights, fisher, members, sketch):
    member_mask = members.astype(jnp.float32)
    folded = exp_size == 4 and weights.shape[1] == 24 * UNIT
    merge = merge_folded if folded else merge_spread
    base, delta, first = merge(weights, fisher, member_mask, sketch, col_size)
    side = lax.rem(lax.axis_index("col"), 2)[None]
    mine, others = sum_halves(*power_step(side, first, delta), col_size)
    basis, coeff = project(side, mine, others, delta)
    return base, basis, coeff


def solution(mesh):
    in_specs = (
        P(("grp", "exp"), None, "col"),
        P(("grp", "exp"), None),
        P("grp", None),
        P(("grp", "exp"), "col", None),
    )
    out_specs = (
        P("grp", "exp", "col"),
        P(("grp", "exp"), None, None),
        P(("grp", "exp"), None, "col"),
    )
    run = functools.partial(body, mesh.shape["exp"], mesh.shape["col"])
    return jax.shard_map(run, mesh=mesh, in_specs=in_specs, out_specs=out_specs, check_vma=False)
```

```python
import functools
import math

import jax
import jax.numpy as jnp
from jax import lax
from jax.experimental import pallas as pl
from jax.experimental.pallas import tpu as pltpu
from jax.sharding import PartitionSpec as P

HIGH = lax.Precision.HIGHEST
UNIT = 32
VMEM_LIMIT = 20 * 1024 * 1024
SMEM = pl.BlockSpec(memory_space=pltpu.SMEM)


def params():
    return pltpu.CompilerParams(vmem_limit_bytes=VMEM_LIMIT)


COST = pl.CostEstimate(flops=10**10, transcendentals=0, bytes_accessed=1)
ANY = pl.BlockSpec(memory_space=pl.ANY)
HBM = pl.BlockSpec(memory_space=pltpu.HBM)


def in_hbm(array):
    return pltpu.with_memory_space_constraint(array, pltpu.HBM)


def sums_kernel(ahead, inner, mask, w_ref, a_ref, f_ref, *refs):
    experts, rows, cols = w_ref.shape
    out_ref = refs[-2] if ahead else refs[-1]
    if ahead:

        @pl.when(inner[0] == 0)
        def _():
            refs[-1][...] = refs[0][...]

    @pl.when(inner[0] == 1)
    def _():
        clusters = out_ref.shape[0]
        strip, width = 16, 512
        across = cols // width

        def one(n, carry):
            r = pl.multiple_of((n // across) * strip, strip)
            c = pl.multiple_of((n % across) * width, width)
            at = (pl.ds(r, strip), pl.ds(c, width))
            totals = [jnp.zeros((strip, width), jnp.float32) for _ in range(clusters)]
            for e in range(2 * experts):
                source = w_ref if e < experts else a_ref
                block = source[e % experts, at[0], at[1]].astype(jnp.float32)
                block = block * f_ref[pl.ds(r, strip), e : e + 1]
                for k in range(clusters):
                    totals[k] = totals[k] + block * mask[e, k]
            for k in range(clusters):
                out_ref[k, at[0], at[1]] = totals[k].astype(jnp.bfloat16)
            return carry

        lax.fori_loop(0, (rows // strip) * across, one, 0)


def cluster_sums(inner, mask, weights, arrived, fcols, start, rows, ahead, after):
    experts, _, cols = weights.shape
    clusters = mask.shape[1]
    first = start // UNIT
    steps = rows // UNIT
    out_specs = [pl.BlockSpec((clusters, UNIT, cols), lambda i, on: (0, i * on[0], 0))]
    out_shape = [jax.ShapeDtypeStruct((clusters, rows, cols), jnp.bfloat16)]
    extra, extra_specs = list(after), [ANY] * len(after)
    if ahead is not None:
        begin, length = ahead
        split = length % (16 * steps) == 0 and begin % (length // steps) == 0
        part = length // steps if split else length
        shape = (experts, part, cols)
        if part != length:
            at = begin // part
            extra_specs.insert(0, pl.BlockSpec(shape, lambda i, on: (0, at + i * (1 - on[0]), 0)))
            out_specs.append(pl.BlockSpec(shape, lambda i, on: (0, i * (1 - on[0]), 0)))
        else:
            place = (pl.Element(experts), pl.Element(length), pl.Element(cols))
            extra_specs.insert(0, pl.BlockSpec(place, lambda i, on: (0, begin, 0)))
            out_specs.append(pl.BlockSpec(shape, lambda i, on: (0, 0, 0)))
        out_shape.append(jax.ShapeDtypeStruct((experts, length, cols), jnp.bfloat16))
        extra.insert(0, in_hbm(weights))
    return pl.pallas_call(
        functools.partial(sums_kernel, ahead is not None),
        grid_spec=pltpu.PrefetchScalarGridSpec(
            num_scalar_prefetch=1,
            grid=(steps,),
            in_specs=[
                SMEM,
                pl.BlockSpec((experts, UNIT, cols), lambda i, on: (0, first + i * on[0], 0)),
                pl.BlockSpec((experts, UNIT, cols), lambda i, on: (0, i * on[0], 0)),
                pl.BlockSpec((UNIT, fcols.shape[1]), lambda i, on: (first + i * on[0], 0)),
            ]
            + extra_specs,
            out_specs=out_specs,
        ),
        out_shape=out_shape,
        cost_estimate=COST,
        compiler_params=params(),
    )(inner, mask, in_hbm(weights), arrived, fcols, *extra)


def base_kernel(inner, labels, p_ref, q_ref, d_ref, *refs):
    clusters, rows, cols = p_ref.shape
    out_ref, chosen_ref = refs[-2:] if labels is not None else (refs[-1], None)

    @pl.when(inner[0] == 1)
    def _():
        scale = 1.0 / d_ref[...]
        for k in range(clusters):
            total = p_ref[k].astype(jnp.float32) + q_ref[k].astype(jnp.float32)
            out_ref[k] = (total * scale[:, k : k + 1]).astype(jnp.bfloat16)
        if chosen_ref is not None:
            for e in range(chosen_ref.shape[0]):
                chosen_ref[e] = out_ref[labels[e]]


def whole_base_kernel(inner, *refs):
    base_kernel(inner, None, *refs)


def make_base(inner, mine, other, denom, start, labels, after):
    clusters, rows, cols = mine.shape
    first = start // UNIT
    block = lambda lead: pl.BlockSpec((lead, UNIT, cols), lambda i, on: (0, i * on[0], 0))
    in_specs = [
        block(clusters),
        block(clusters),
        pl.BlockSpec((UNIT, clusters), lambda i, on: (first + i * on[0], 0)),
    ]
    shape = jax.ShapeDtypeStruct(mine.shape, jnp.bfloat16)
    kernel, operands, outs, shapes = whole_base_kernel, (), block(clusters), shape
    if labels is not None:
        kernel, operands = base_kernel, (labels,)
        in_specs = [SMEM] + in_specs
        experts = labels.shape[0]
        outs = [block(clusters), block(experts)]
        shapes = [shape, jax.ShapeDtypeStruct((experts, rows, cols), jnp.bfloat16)]
    return pl.pallas_call(
        kernel,
        grid_spec=pltpu.PrefetchScalarGridSpec(
            num_scalar_prefetch=1,
            grid=(rows // UNIT,),
            in_specs=in_specs + [ANY] * len(after),
            out_specs=outs,
        ),
        out_shape=shapes,
        cost_estimate=COST,
        compiler_params=params(),
    )(inner, *operands, mine, other, denom, *after)


def residual_kernel(meta, w_ref, b_ref, r_ref, s_ref, *refs):
    delta_ref, base_ref, first_ref = refs[-3:]
    experts = w_ref.shape[0]
    by_expert = r_ref.shape[0] == experts
    inner = meta[experts] == 1
    labels = [meta[e] for e in range(experts)]
    base_ref[...] = b_ref[...] if by_expert else r_ref[...]

    def subtract(source, indices):
        for e in range(experts):
            chosen = source[indices[e]].astype(jnp.float32)
            delta_ref[e] = (w_ref[e].astype(jnp.float32) - chosen).astype(jnp.bfloat16)

    @pl.when(inner)
    def _():
        subtract(b_ref, labels)

    @pl.when(jnp.logical_not(inner))
    def _():
        subtract(r_ref, range(experts) if by_expert else labels)

    for e in range(experts):
        first_ref[e] = jnp.dot(delta_ref[e], s_ref[e], preferred_element_type=jnp.float32)


def residual_chunk(meta, weights, base, arrived, sketch, quarter, start, held, after):
    experts, units, cols = weights.shape
    clusters, rows, _ = base.shape
    rank = sketch.shape[2]
    first = start // UNIT
    quarter_blocks = units // 4 // UNIT
    local = first - quarter * quarter_blocks
    own = lambda meta: meta[experts + 1] == quarter

    def keep(i, meta):
        return (0, jnp.where(own(meta), local + i, quarter_blocks), 0)

    chunk = lambda lead: pl.BlockSpec((lead, UNIT, cols), lambda i, meta: (0, i, 0))
    placed = pl.BlockSpec((experts, UNIT, cols), lambda i, meta: (0, first + i, 0))
    return pl.pallas_call(
        residual_kernel,
        grid_spec=pltpu.PrefetchScalarGridSpec(
            num_scalar_prefetch=1,
            grid=(rows // UNIT,),
            in_specs=[
                placed,
                chunk(clusters),
                chunk(arrived.shape[0]),
                pl.BlockSpec(sketch.shape, lambda i, meta: (0, 0, 0)),
            ]
            + [HBM] * len(held)
            + [ANY] * len(after),
            out_specs=[
                placed,
                pl.BlockSpec((clusters, UNIT, cols), keep),
                pl.BlockSpec((experts, UNIT, rank), lambda i, meta: (0, i, 0)),
            ],
        ),
        out_shape=[
            pltpu.HBM((experts, units, cols), jnp.bfloat16),
            pltpu.HBM((clusters, units // 4 + UNIT, cols), jnp.bfloat16),
            jax.ShapeDtypeStruct((experts, rows, rank), jnp.float32),
        ],
        cost_estimate=COST,
        input_output_aliases={5 + i: i for i in range(len(held))},
        compiler_params=params(),
    )(meta, in_hbm(weights), base, arrived, sketch, *held, *after)


def copy_kernel(in_ref, out_ref):
    out_ref[...] = in_ref[...]


def leading_rows(array, rows):
    lead, _, cols = array.shape
    block = pl.BlockSpec((lead, rows, cols // 2), lambda i: (0, 0, i))
    return pl.pallas_call(
        copy_kernel,
        grid=(2,),
        in_specs=[block],
        out_specs=block,
        out_shape=jax.ShapeDtypeStruct((lead, rows, cols), array.dtype),
        compiler_params=params(),
    )(array)


GROUP = 8


def inverse_factors(grams):
    size = grams[0].shape[0]
    lane = lax.broadcasted_iota(jnp.int32, (GROUP, size), 1)
    sub = lax.broadcasted_iota(jnp.int32, (GROUP, size), 0)
    groups = range(size // GROUP)
    tables = [[g[i * GROUP : (i + 1) * GROUP] for i in groups] for g in grams]
    for at in groups:
        first = at * GROUP
        block = (lane >= first) & (lane < first + GROUP)
        unit = jnp.where(lane - first == sub, 1.0, 0.0)
        for table in tables:
            own = table[at]
            cols = [
                jnp.broadcast_to(own[:, first + t : first + t + 1], (GROUP, size))
                for t in range(GROUP)
            ]
            rows = jnp.where(block, unit, own)
            diag = cols[0]
            for t in range(GROUP - 1):
                factor = jnp.where(sub > t, cols[t] * (1.0 / cols[t][t : t + 1]), 0.0)
                for s in range(t + 1, GROUP):
                    cols[s] = cols[s] - factor * cols[s][t : t + 1]
                rows = rows - factor * rows[t : t + 1]
                diag = jnp.where(sub > t, cols[t + 1], diag)
            inverse = 1.0 / diag
            table[at] = rows * lax.rsqrt(diag)
            solved = rows * inverse
            for t in range(GROUP - 1, 0, -1):
                upper = jnp.where(sub < t, cols[t] * inverse, 0.0)
                solved = solved - upper * solved[t : t + 1]
            for i in range(at + 1, size // GROUP):
                value = table[i]
                rest = jnp.where(block, 0.0, value)
                for t in range(GROUP):
                    col = jnp.broadcast_to(value[:, first + t : first + t + 1], (GROUP, size))
                    rest = rest - col * solved[t : t + 1]
                table[i] = rest
    out = []
    for table in tables:
        parts = [jnp.where(lane <= sub + i * GROUP, table[i], 0.0) for i in groups]
        out.append(jnp.concatenate(parts, axis=0))
    return out


def contract(left, right, dims, precision=None):
    return lax.dot_general(
        left, right, (dims, ((), ())), precision=precision, preferred_element_type=jnp.float32
    )


def ranges(values, units):
    grams = [contract(y, y, ((0,), (0,)), HIGH) for y in values]
    factors = inverse_factors(grams)
    return [
        (contract(y, m, ((1,), (1,)), HIGH) * math.sqrt(units)).astype(jnp.bfloat16)
        for y, m in zip(values, factors)
    ]


def power_kernel(splits, pieces, side, *refs):
    parts = refs[: sum(splits)]
    delta_ref = refs[sum(splits)]
    keep_ref, send_ref, value, held, sem = refs[-5:]
    experts, units, _ = delta_ref.shape
    half = units // 2
    copy = pltpu.make_async_copy(delta_ref, held, sem)
    copy.start()
    at = 0
    for count, places in zip(splits, pieces):
        total = parts[at][...].astype(jnp.float32)
        for part in parts[at + 1 : at + count]:
            total = total + part[...].astype(jnp.float32)
        row = 0
        for start, rows in places:
            value[:, start : start + rows] = total[:, row : row + rows]
            row += rows
        at = at + count
    start = ranges([value[e] for e in range(experts)], units)
    copy.wait()
    own = pl.multiple_of(side[0] * half, half)
    other = pl.multiple_of((1 - side[0]) * half, half)
    for e in range(experts):
        back = contract(start[e], held[e], ((0,), (0,))).astype(jnp.bfloat16)
        keep_ref[e] = contract(held[e, pl.ds(own, half)], back, ((1,), (1,)))
        send_ref[e] = contract(held[e, pl.ds(other, half)], back, ((1,), (1,)))


def power_step(side, groups, delta):
    experts, units, _ = delta.shape
    pieces, groups = zip(*groups)
    rank = groups[0][0].shape[2]
    part = jax.ShapeDtypeStruct((experts, units // 2, rank), jnp.float32)
    vmem = pl.BlockSpec(memory_space=pltpu.VMEM)
    splits = tuple(len(g) for g in groups)
    return pl.pallas_call(
        functools.partial(power_kernel, splits, pieces),
        in_specs=[SMEM] + [vmem] * sum(splits) + [HBM],
        out_specs=[vmem] * 2,
        out_shape=[part, part],
        scratch_shapes=[
            pltpu.VMEM((experts, units, rank), jnp.float32),
            pltpu.VMEM(delta.shape, jnp.bfloat16),
            pltpu.SemaphoreType.DMA,
        ],
        compiler_params=params(),
    )(side, *[term for g in groups for term in g], delta)


def project_kernel(side, *refs):
    parts, (delta_ref, basis_ref, coeff_ref, value, held, sem) = refs[:-6], refs[-6:]
    experts, half, _ = parts[0].shape
    units = 2 * half
    copy = pltpu.make_async_copy(delta_ref, held, sem)
    copy.start()
    count = len(parts) // 2
    for place, group in ((side[0], parts[:count]), (1 - side[0], parts[count:])):
        total = group[0][...].astype(jnp.float32)
        for part in group[1:]:
            total = total + part[...].astype(jnp.float32)
        value[:, pl.ds(pl.multiple_of(place * half, half), half)] = total
    basis = ranges([value[e] for e in range(experts)], units)
    copy.wait()
    for e in range(experts):
        basis_ref[e] = basis[e]
        coeff = contract(basis[e], held[e], ((0,), (0,)))
        coeff_ref[e] = (coeff * (1.0 / math.sqrt(units))).astype(jnp.bfloat16)


def project(side, mine, others, delta):
    experts, units, _ = delta.shape
    rank = mine[0].shape[2]
    vmem = pl.BlockSpec(memory_space=pltpu.VMEM)
    return pl.pallas_call(
        project_kernel,
        in_specs=[SMEM] + [vmem] * (len(mine) + len(others)) + [HBM],
        out_specs=[vmem] * 2,
        out_shape=[
            jax.ShapeDtypeStruct((experts, units, rank), jnp.bfloat16),
            jax.ShapeDtypeStruct((experts, rank, delta.shape[2]), jnp.bfloat16),
        ],
        scratch_shapes=[
            pltpu.VMEM((experts, units, rank), jnp.float32),
            pltpu.VMEM(delta.shape, jnp.bfloat16),
            pltpu.SemaphoreType.DMA,
        ],
        compiler_params=params(),
    )(side, *mine, *others, delta)


def swap(value, bit, size):
    return lax.ppermute(value, "col", [(i, i ^ bit) for i in range(size)])


def sum_columns(value, size):
    bit = 1
    while 2 * bit < size:
        value = value + swap(value, bit, size)
        bit *= 2
    value = value.astype(jnp.bfloat16)
    return value, swap(value, bit, size)


def sum_halves(keep, send, size):
    total = (keep + swap(send, 1, size)).astype(jnp.bfloat16)
    bit = 2
    while 2 * bit < size:
        total = (total.astype(jnp.float32) + swap(total, bit, size).astype(jnp.float32)).astype(
            jnp.bfloat16
        )
        bit *= 2
    far = swap(total, bit, size)
    return (total, far), (swap(total, 1, size), swap(far, 1, size))


def merge_folded(weights, fisher, member_mask, sketch, col_size):
    inwards, across, outwards = [(0, 1), (3, 2)], [(1, 2), (2, 1)], [(1, 0), (2, 3)]
    experts, units, cols = weights.shape
    clusters = member_mask.shape[1]
    place = lax.axis_index("exp")
    inner = ((place == 1) | (place == 2)).astype(jnp.int32)[None]
    mine = lax.dynamic_slice_in_dim(member_mask, place * experts, experts)
    partner = lax.dynamic_slice_in_dim(member_mask, (place ^ 1) * experts, experts)
    mask = jnp.concatenate([mine, partner], axis=0)
    meta = jnp.concatenate([jnp.argmax(mine, axis=1).astype(jnp.int32), inner, place[None]])
    near = [fisher.astype(jnp.float32)]
    for hop in (1, 2, 3):
        pairs = [(i, i ^ hop) for i in range(4)]
        near.append(lax.ppermute(fisher, "exp", pairs).astype(jnp.float32))
    denom = jnp.zeros((units, clusters), jnp.float32)
    for hop, value in enumerate(near):
        rows = lax.dynamic_slice_in_dim(member_mask, (place ^ hop) * experts, experts)
        denom = denom + jnp.sum(value[:, :, None] * rows[:, None, :], axis=0)
    fcols = jnp.concatenate(near[:2], axis=0).T

    chunks = [(0, 2), (0, 2), (0, 2), (3, 3), (3, 3), (1, 3), (1, 3), (2, 3), (2, 2), (2, 1)]
    groups = [(0, 1, 2, 3, 4), (5, 6, 7), (8, 9)]
    lead, lag = 2, 2
    spans, used = [], [0] * 4
    for q, size in chunks:
        spans.append((q * (units // 4) + used[q], size * UNIT))
        used[q] += size * UNIT
    count = len(chunks)
    their_labels = jnp.argmax(partner, axis=1).astype(jnp.int32)
    arrived, sums, others, base, moved, firsts = {}, {}, {}, {}, {}, {}
    held, after, terms, ready = (), (), [], {}
    for c in range(lead):
        block = weights[:, spans[c][0] : sum(spans[c])]
        arrived[c] = lax.ppermute(block, "exp", inwards)
    order = []
    for step in range(count):
        order += [("sums", step), ("base", step - 1), ("residual", step - lag)]
    order += [("base", count - 1)] + [("residual", c) for c in range(count - lag, count)]
    for kind, c in order:
        if c < 0:
            continue
        if kind == "sums":
            ahead = spans[c + lead] if c + lead < count else None
            sums[c], *copied = cluster_sums(
                inner, mask, weights, arrived[c], fcols, *spans[c], ahead, after
            )
            others[c] = lax.ppermute(sums[c], "exp", across)
            if copied:
                arrived[c + lead] = lax.ppermute(copied[0], "exp", inwards)
            after = (sums[c],)
        elif kind == "base":
            whole = chunks[c][0] in (0, 3)
            labels = None if whole else their_labels
            result = make_base(inner, sums[c], others[c], denom, spans[c][0], labels, after)
            base[c], leaving = (result, result) if whole else result
            moved[c] = lax.ppermute(leaving, "exp", outwards)
            after = (base[c],)
        else:
            if c == count - 2:
                after = after + (moved[count - 1],)
            *held, firsts[c] = residual_chunk(
                meta,
                weights,
                base[c],
                moved[c],
                sketch,
                chunks[c][0],
                spans[c][0],
                held,
                after + ready.pop(c, ()),
            )
            after = (firsts[c],)
            for group in groups:
                if c == group[-1]:
                    joined = jnp.concatenate([firsts[g] for g in group], axis=1)
                    total = sum_columns(joined, col_size)
                    terms.append((tuple(spans[g] for g in group), total))
                    ready[c + 2] = total[1:]
    delta, bases = held
    base = leading_rows(bases, units // 4)
    return base, delta, terms


def merge_spread(weights, fisher, member_mask, sketch, col_size):
    moved = lax.all_to_all(weights, "exp", split_axis=1, concat_axis=0, tiled=True)
    f_rows = lax.all_to_all(fisher, "exp", split_axis=1, concat_axis=0, tiled=True)
    f_wide = f_rows.astype(jnp.float32)
    weighted = f_wide[:, :, None] * moved.astype(jnp.float32)
    numer = jnp.einsum("ek,erc->krc", member_mask, weighted, precision=HIGH)
    denom = jnp.einsum("ek,er->kr", member_mask, f_wide, precision=HIGH)
    base = (numer / denom[:, :, None]).astype(jnp.bfloat16)
    chosen = jnp.take(base, jnp.argmax(member_mask, axis=1), axis=0)
    residual = (moved.astype(jnp.float32) - chosen.astype(jnp.float32)).astype(jnp.bfloat16)
    delta = lax.all_to_all(residual, "exp", split_axis=0, concat_axis=1, tiled=True)
    first = jnp.einsum("nrc,nck->nrk", delta, sketch, preferred_element_type=jnp.float32)
    return base, delta, [(((0, first.shape[1]),), sum_columns(first, col_size))]


def body(exp_size, col_size, weights, fisher, members, sketch):
    member_mask = members.astype(jnp.float32)
    folded = exp_size == 4 and weights.shape[1] == 24 * UNIT
    merge = merge_folded if folded else merge_spread
    base, delta, first = merge(weights, fisher, member_mask, sketch, col_size)
    side = lax.rem(lax.axis_index("col"), 2)[None]
    mine, others = sum_halves(*power_step(side, first, delta), col_size)
    basis, coeff = project(side, mine, others, delta)
    return base, basis, coeff


def solution(mesh):
    in_specs = (
        P(("grp", "exp"), None, "col"),
        P(("grp", "exp"), None),
        P("grp", None),
        P(("grp", "exp"), "col", None),
    )
    out_specs = (
        P("grp", "exp", "col"),
        P(("grp", "exp"), None, None),
        P(("grp", "exp"), None, "col"),
    )
    run = functools.partial(body, mesh.shape["exp"], mesh.shape["col"])
    return jax.shard_map(run, mesh=mesh, in_specs=in_specs, out_specs=out_specs, check_vma=False)
```

```python
import functools
import math

import jax
import jax.numpy as jnp
from jax import lax
from jax.experimental import pallas as pl
from jax.experimental.pallas import tpu as pltpu
from jax.sharding import PartitionSpec as P

HIGH = lax.Precision.HIGHEST
UNIT = 32
VMEM_LIMIT = 20 * 1024 * 1024
SMEM = pl.BlockSpec(memory_space=pltpu.SMEM)


def params():
    return pltpu.CompilerParams(vmem_limit_bytes=VMEM_LIMIT)


COST = pl.CostEstimate(flops=10**10, transcendentals=0, bytes_accessed=1)
ANY = pl.BlockSpec(memory_space=pl.ANY)
HBM = pl.BlockSpec(memory_space=pltpu.HBM)


def in_hbm(array):
    return pltpu.with_memory_space_constraint(array, pltpu.HBM)


def sums_kernel(ahead, inner, mask, w_ref, a_ref, f_ref, *refs):
    experts, rows, cols = w_ref.shape
    out_ref = refs[-2] if ahead else refs[-1]
    if ahead:

        @pl.when(inner[0] == 0)
        def _():
            refs[-1][...] = refs[0][...]

    @pl.when(inner[0] == 1)
    def _():
        clusters = out_ref.shape[0]
        strip, width = 16, 512
        across = cols // width

        def one(n, carry):
            r = pl.multiple_of((n // across) * strip, strip)
            c = pl.multiple_of((n % across) * width, width)
            at = (pl.ds(r, strip), pl.ds(c, width))
            totals = [jnp.zeros((strip, width), jnp.float32) for _ in range(clusters)]
            for e in range(2 * experts):
                source = w_ref if e < experts else a_ref
                block = source[e % experts, at[0], at[1]].astype(jnp.float32)
                block = block * f_ref[pl.ds(r, strip), e : e + 1]
                for k in range(clusters):
                    totals[k] = totals[k] + block * mask[e, k]
            for k in range(clusters):
                out_ref[k, at[0], at[1]] = totals[k].astype(jnp.bfloat16)
            return carry

        lax.fori_loop(0, (rows // strip) * across, one, 0)


def cluster_sums(inner, mask, weights, arrived, fcols, start, rows, ahead, after):
    experts, _, cols = weights.shape
    clusters = mask.shape[1]
    first = start // UNIT
    steps = rows // UNIT
    out_specs = [pl.BlockSpec((clusters, UNIT, cols), lambda i, on: (0, i * on[0], 0))]
    out_shape = [jax.ShapeDtypeStruct((clusters, rows, cols), jnp.bfloat16)]
    extra, extra_specs = list(after), [ANY] * len(after)
    if ahead is not None:
        begin, length = ahead
        split = length % (16 * steps) == 0 and begin % (length // steps) == 0
        part = length // steps if split else length
        shape = (experts, part, cols)
        if part != length:
            at = begin // part
            extra_specs.insert(0, pl.BlockSpec(shape, lambda i, on: (0, at + i * (1 - on[0]), 0)))
            out_specs.append(pl.BlockSpec(shape, lambda i, on: (0, i * (1 - on[0]), 0)))
        else:
            place = (pl.Element(experts), pl.Element(length), pl.Element(cols))
            extra_specs.insert(0, pl.BlockSpec(place, lambda i, on: (0, begin, 0)))
            out_specs.append(pl.BlockSpec(shape, lambda i, on: (0, 0, 0)))
        out_shape.append(jax.ShapeDtypeStruct((experts, length, cols), jnp.bfloat16))
        extra.insert(0, in_hbm(weights))
    return pl.pallas_call(
        functools.partial(sums_kernel, ahead is not None),
        grid_spec=pltpu.PrefetchScalarGridSpec(
            num_scalar_prefetch=1,
            grid=(steps,),
            in_specs=[
                SMEM,
                pl.BlockSpec((experts, UNIT, cols), lambda i, on: (0, first + i * on[0], 0)),
                pl.BlockSpec((experts, UNIT, cols), lambda i, on: (0, i * on[0], 0)),
                pl.BlockSpec((UNIT, fcols.shape[1]), lambda i, on: (first + i * on[0], 0)),
            ]
            + extra_specs,
            out_specs=out_specs,
        ),
        out_shape=out_shape,
        cost_estimate=COST,
        compiler_params=params(),
    )(inner, mask, in_hbm(weights), arrived, fcols, *extra)


def base_kernel(inner, labels, p_ref, q_ref, d_ref, *refs):
    clusters, rows, cols = p_ref.shape
    out_ref, chosen_ref = refs[-2:] if labels is not None else (refs[-1], None)

    @pl.when(inner[0] == 1)
    def _():
        scale = 1.0 / d_ref[...]
        for k in range(clusters):
            total = p_ref[k].astype(jnp.float32) + q_ref[k].astype(jnp.float32)
            out_ref[k] = (total * scale[:, k : k + 1]).astype(jnp.bfloat16)
        if chosen_ref is not None:
            for e in range(chosen_ref.shape[0]):
                chosen_ref[e] = out_ref[labels[e]]


def whole_base_kernel(inner, *refs):
    base_kernel(inner, None, *refs)


def make_base(inner, mine, other, denom, start, labels, after):
    clusters, rows, cols = mine.shape
    first = start // UNIT
    block = lambda lead: pl.BlockSpec((lead, UNIT, cols), lambda i, on: (0, i * on[0], 0))
    in_specs = [
        block(clusters),
        block(clusters),
        pl.BlockSpec((UNIT, clusters), lambda i, on: (first + i * on[0], 0)),
    ]
    shape = jax.ShapeDtypeStruct(mine.shape, jnp.bfloat16)
    kernel, operands, outs, shapes = whole_base_kernel, (), block(clusters), shape
    if labels is not None:
        kernel, operands = base_kernel, (labels,)
        in_specs = [SMEM] + in_specs
        experts = labels.shape[0]
        outs = [block(clusters), block(experts)]
        shapes = [shape, jax.ShapeDtypeStruct((experts, rows, cols), jnp.bfloat16)]
    return pl.pallas_call(
        kernel,
        grid_spec=pltpu.PrefetchScalarGridSpec(
            num_scalar_prefetch=1,
            grid=(rows // UNIT,),
            in_specs=in_specs + [ANY] * len(after),
            out_specs=outs,
        ),
        out_shape=shapes,
        cost_estimate=COST,
        compiler_params=params(),
    )(inner, *operands, mine, other, denom, *after)


def residual_kernel(meta, w_ref, b_ref, r_ref, s_ref, *refs):
    delta_ref, base_ref, first_ref = refs[-3:]
    experts = w_ref.shape[0]
    by_expert = r_ref.shape[0] == experts
    inner = meta[experts] == 1
    labels = [meta[e] for e in range(experts)]
    base_ref[...] = b_ref[...] if by_expert else r_ref[...]

    def subtract(source, indices):
        for e in range(experts):
            chosen = source[indices[e]].astype(jnp.float32)
            delta_ref[e] = (w_ref[e].astype(jnp.float32) - chosen).astype(jnp.bfloat16)

    @pl.when(inner)
    def _():
        subtract(b_ref, labels)

    @pl.when(jnp.logical_not(inner))
    def _():
        subtract(r_ref, range(experts) if by_expert else labels)

    for e in range(experts):
        first_ref[e] = jnp.dot(delta_ref[e], s_ref[e], preferred_element_type=jnp.float32)


def residual_chunk(meta, weights, base, arrived, sketch, quarter, start, held, after):
    experts, units, cols = weights.shape
    clusters, rows, _ = base.shape
    rank = sketch.shape[2]
    first = start // UNIT
    quarter_blocks = units // 4 // UNIT
    local = first - quarter * quarter_blocks
    own = lambda meta: meta[experts + 1] == quarter

    def keep(i, meta):
        return (0, jnp.where(own(meta), local + i, quarter_blocks), 0)

    chunk = lambda lead: pl.BlockSpec((lead, UNIT, cols), lambda i, meta: (0, i, 0))
    placed = pl.BlockSpec((experts, UNIT, cols), lambda i, meta: (0, first + i, 0))
    return pl.pallas_call(
        residual_kernel,
        grid_spec=pltpu.PrefetchScalarGridSpec(
            num_scalar_prefetch=1,
            grid=(rows // UNIT,),
            in_specs=[
                placed,
                chunk(clusters),
                chunk(arrived.shape[0]),
                pl.BlockSpec(sketch.shape, lambda i, meta: (0, 0, 0)),
            ]
            + [HBM] * len(held)
            + [ANY] * len(after),
            out_specs=[
                placed,
                pl.BlockSpec((clusters, UNIT, cols), keep),
                pl.BlockSpec((experts, UNIT, rank), lambda i, meta: (0, i, 0)),
            ],
        ),
        out_shape=[
            pltpu.HBM((experts, units, cols), jnp.bfloat16),
            pltpu.HBM((clusters, units // 4 + UNIT, cols), jnp.bfloat16),
            jax.ShapeDtypeStruct((experts, rows, rank), jnp.float32),
        ],
        cost_estimate=COST,
        input_output_aliases={5 + i: i for i in range(len(held))},
        compiler_params=params(),
    )(meta, in_hbm(weights), base, arrived, sketch, *held, *after)


def copy_kernel(in_ref, out_ref):
    out_ref[...] = in_ref[...]


def leading_rows(array, rows):
    lead, _, cols = array.shape
    block = pl.BlockSpec((lead, rows, cols // 2), lambda i: (0, 0, i))
    return pl.pallas_call(
        copy_kernel,
        grid=(2,),
        in_specs=[block],
        out_specs=block,
        out_shape=jax.ShapeDtypeStruct((lead, rows, cols), array.dtype),
        compiler_params=params(),
    )(array)


GROUP = 8


def inverse_factors(grams):
    size = grams[0].shape[0]
    lane = lax.broadcasted_iota(jnp.int32, (GROUP, size), 1)
    sub = lax.broadcasted_iota(jnp.int32, (GROUP, size), 0)
    groups = range(size // GROUP)
    tables = [[g[i * GROUP : (i + 1) * GROUP] for i in groups] for g in grams]
    for at in groups:
        first = at * GROUP
        block = (lane >= first) & (lane < first + GROUP)
        unit = jnp.where(lane - first == sub, 1.0, 0.0)
        for table in tables:
            own = table[at]
            cols = [
                jnp.broadcast_to(own[:, first + t : first + t + 1], (GROUP, size))
                for t in range(GROUP)
            ]
            rows = jnp.where(block, unit, own)
            diag = cols[0]
            for t in range(GROUP - 1):
                factor = jnp.where(sub > t, cols[t] * (1.0 / cols[t][t : t + 1]), 0.0)
                for s in range(t + 1, GROUP):
                    cols[s] = cols[s] - factor * cols[s][t : t + 1]
                rows = rows - factor * rows[t : t + 1]
                diag = jnp.where(sub > t, cols[t + 1], diag)
            inverse = 1.0 / diag
            table[at] = rows * lax.rsqrt(diag)
            solved = rows * inverse
            for t in range(GROUP - 1, 0, -1):
                upper = jnp.where(sub < t, cols[t] * inverse, 0.0)
                solved = solved - upper * solved[t : t + 1]
            for i in range(at + 1, size // GROUP):
                value = table[i]
                rest = jnp.where(block, 0.0, value)
                for t in range(GROUP):
                    col = jnp.broadcast_to(value[:, first + t : first + t + 1], (GROUP, size))
                    rest = rest - col * solved[t : t + 1]
                table[i] = rest
    out = []
    for table in tables:
        parts = [jnp.where(lane <= sub + i * GROUP, table[i], 0.0) for i in groups]
        out.append(jnp.concatenate(parts, axis=0))
    return out


def contract(left, right, dims, precision=None):
    return lax.dot_general(
        left, right, (dims, ((), ())), precision=precision, preferred_element_type=jnp.float32
    )


def ranges(values, units):
    grams = [contract(y, y, ((0,), (0,)), HIGH) for y in values]
    factors = inverse_factors(grams)
    return [
        (contract(y, m, ((1,), (1,)), HIGH) * math.sqrt(units)).astype(jnp.bfloat16)
        for y, m in zip(values, factors)
    ]


def power_kernel(splits, pieces, side, *refs):
    parts = refs[: sum(splits)]
    delta_ref = refs[sum(splits)]
    keep_ref, send_ref, value, held, sem = refs[-5:]
    experts, units, _ = delta_ref.shape
    half = units // 2
    copy = pltpu.make_async_copy(delta_ref, held, sem)
    copy.start()
    at = 0
    for count, places in zip(splits, pieces):
        total = parts[at][...].astype(jnp.float32)
        for part in parts[at + 1 : at + count]:
            total = total + part[...].astype(jnp.float32)
        row = 0
        for start, rows in places:
            value[:, start : start + rows] = total[:, row : row + rows]
            row += rows
        at = at + count
    start = ranges([value[e] for e in range(experts)], units)
    copy.wait()
    own = pl.multiple_of(side[0] * half, half)
    other = pl.multiple_of((1 - side[0]) * half, half)
    for e in range(experts):
        back = contract(start[e], held[e], ((0,), (0,))).astype(jnp.bfloat16)
        keep_ref[e] = contract(held[e, pl.ds(own, half)], back, ((1,), (1,)))
        send_ref[e] = contract(held[e, pl.ds(other, half)], back, ((1,), (1,)))


def power_step(side, groups, delta):
    experts, units, _ = delta.shape
    pieces, groups = zip(*groups)
    rank = groups[0][0].shape[2]
    part = jax.ShapeDtypeStruct((experts, units // 2, rank), jnp.float32)
    vmem = pl.BlockSpec(memory_space=pltpu.VMEM)
    splits = tuple(len(g) for g in groups)
    return pl.pallas_call(
        functools.partial(power_kernel, splits, pieces),
        in_specs=[SMEM] + [vmem] * sum(splits) + [HBM],
        out_specs=[vmem] * 2,
        out_shape=[part, part],
        scratch_shapes=[
            pltpu.VMEM((experts, units, rank), jnp.float32),
            pltpu.VMEM(delta.shape, jnp.bfloat16),
            pltpu.SemaphoreType.DMA,
        ],
        compiler_params=params(),
    )(side, *[term for g in groups for term in g], delta)


def project_kernel(side, *refs):
    parts, (delta_ref, basis_ref, coeff_ref, value, held, sem) = refs[:-6], refs[-6:]
    experts, half, _ = parts[0].shape
    units = 2 * half
    copy = pltpu.make_async_copy(delta_ref, held, sem)
    copy.start()
    count = len(parts) // 2
    for place, group in ((side[0], parts[:count]), (1 - side[0], parts[count:])):
        total = group[0][...].astype(jnp.float32)
        for part in group[1:]:
            total = total + part[...].astype(jnp.float32)
        value[:, pl.ds(pl.multiple_of(place * half, half), half)] = total
    basis = ranges([value[e] for e in range(experts)], units)
    copy.wait()
    for e in range(experts):
        basis_ref[e] = basis[e]
        coeff = contract(basis[e], held[e], ((0,), (0,)))
        coeff_ref[e] = (coeff * (1.0 / math.sqrt(units))).astype(jnp.bfloat16)


def project(side, mine, others, delta):
    experts, units, _ = delta.shape
    rank = mine[0].shape[2]
    vmem = pl.BlockSpec(memory_space=pltpu.VMEM)
    return pl.pallas_call(
        project_kernel,
        in_specs=[SMEM] + [vmem] * (len(mine) + len(others)) + [HBM],
        out_specs=[vmem] * 2,
        out_shape=[
            jax.ShapeDtypeStruct((experts, units, rank), jnp.bfloat16),
            jax.ShapeDtypeStruct((experts, rank, delta.shape[2]), jnp.bfloat16),
        ],
        scratch_shapes=[
            pltpu.VMEM((experts, units, rank), jnp.float32),
            pltpu.VMEM(delta.shape, jnp.bfloat16),
            pltpu.SemaphoreType.DMA,
        ],
        compiler_params=params(),
    )(side, *mine, *others, delta)


def swap(value, bit, size):
    return lax.ppermute(value, "col", [(i, i ^ bit) for i in range(size)])


def sum_columns(value, size):
    bit = 1
    while 2 * bit < size:
        value = value + swap(value, bit, size)
        bit *= 2
    value = value.astype(jnp.bfloat16)
    return value, swap(value, bit, size)


def sum_halves(keep, send, size):
    total = (keep + swap(send, 1, size)).astype(jnp.bfloat16)
    bit = 2
    while 2 * bit < size:
        total = (total.astype(jnp.float32) + swap(total, bit, size).astype(jnp.float32)).astype(
            jnp.bfloat16
        )
        bit *= 2
    far = swap(total, bit, size)
    return (total, far), (swap(total, 1, size), swap(far, 1, size))


def merge_folded(weights, fisher, member_mask, sketch, col_size):
    inwards, across, outwards = [(0, 1), (3, 2)], [(1, 2), (2, 1)], [(1, 0), (2, 3)]
    experts, units, cols = weights.shape
    clusters = member_mask.shape[1]
    place = lax.axis_index("exp")
    inner = ((place == 1) | (place == 2)).astype(jnp.int32)[None]
    mine = lax.dynamic_slice_in_dim(member_mask, place * experts, experts)
    partner = lax.dynamic_slice_in_dim(member_mask, (place ^ 1) * experts, experts)
    mask = jnp.concatenate([mine, partner], axis=0)
    meta = jnp.concatenate([jnp.argmax(mine, axis=1).astype(jnp.int32), inner, place[None]])
    opening = weights[:, : UNIT]
    fisher, opening = lax.optimization_barrier((fisher, opening))
    near = [fisher.astype(jnp.float32)]
    for hop in (1, 2, 3):
        pairs = [(i, i ^ hop) for i in range(4)]
        near.append(lax.ppermute(fisher, "exp", pairs).astype(jnp.float32))
    denom = jnp.zeros((units, clusters), jnp.float32)
    for hop, value in enumerate(near):
        rows = lax.dynamic_slice_in_dim(member_mask, (place ^ hop) * experts, experts)
        denom = denom + jnp.sum(value[:, :, None] * rows[:, None, :], axis=0)
    fcols = jnp.concatenate(near[:2], axis=0).T

    chunks = [(0, 1), (0, 2), (0, 3), (3, 3), (3, 3), (1, 3), (1, 3), (2, 2), (2, 2), (2, 2)]
    groups = [(0, 1, 2, 3, 4), (5, 6, 7), (8, 9)]
    lead, lag = 2, 2
    spans, used = [], [0] * 4
    for q, size in chunks:
        spans.append((q * (units // 4) + used[q], size * UNIT))
        used[q] += size * UNIT
    count = len(chunks)
    their_labels = jnp.argmax(partner, axis=1).astype(jnp.int32)
    arrived, sums, others, base, moved, firsts = {}, {}, {}, {}, {}, {}
    held, after, terms, ready = (), (), [], {}
    for c in range(lead):
        block = weights[:, spans[c][0] : sum(spans[c])] if c else opening
        arrived[c] = lax.ppermute(block, "exp", inwards)
    order = []
    for step in range(count):
        order += [("sums", step), ("base", step - 1), ("residual", step - lag)]
    order += [("residual", count - 2), ("base", count - 1), ("residual", count - 1)]
    for kind, c in order:
        if c < 0:
            continue
        if kind == "sums":
            ahead = spans[c + lead] if c + lead < count else None
            sums[c], *copied = cluster_sums(
                inner, mask, weights, arrived[c], fcols, *spans[c], ahead, after
            )
            others[c] = lax.ppermute(sums[c], "exp", across)
            if copied:
                arrived[c + lead] = lax.ppermute(copied[0], "exp", inwards)
            after = (sums[c],)
        elif kind == "base":
            whole = chunks[c][0] in (0, 3)
            labels = None if whole else their_labels
            result = make_base(inner, sums[c], others[c], denom, spans[c][0], labels, after)
            base[c], leaving = (result, result) if whole else result
            moved[c] = lax.ppermute(leaving, "exp", outwards)
            after = (base[c],)
        else:
            *held, firsts[c] = residual_chunk(
                meta,
                weights,
                base[c],
                moved[c],
                sketch,
                chunks[c][0],
                spans[c][0],
                held,
                after + ready.pop(c, ()),
            )
            after = (firsts[c],)
            for group in groups:
                if c == group[-1]:
                    joined = jnp.concatenate([firsts[g] for g in group], axis=1)
                    total = sum_columns(joined, col_size)
                    terms.append((tuple(spans[g] for g in group), total))
                    ready[c + 2] = total[1:]
    delta, bases = held
    base = leading_rows(bases, units // 4)
    return base, delta, terms


def merge_spread(weights, fisher, member_mask, sketch, col_size):
    moved = lax.all_to_all(weights, "exp", split_axis=1, concat_axis=0, tiled=True)
    f_rows = lax.all_to_all(fisher, "exp", split_axis=1, concat_axis=0, tiled=True)
    f_wide = f_rows.astype(jnp.float32)
    weighted = f_wide[:, :, None] * moved.astype(jnp.float32)
    numer = jnp.einsum("ek,erc->krc", member_mask, weighted, precision=HIGH)
    denom = jnp.einsum("ek,er->kr", member_mask, f_wide, precision=HIGH)
    base = (numer / denom[:, :, None]).astype(jnp.bfloat16)
    chosen = jnp.take(base, jnp.argmax(member_mask, axis=1), axis=0)
    residual = (moved.astype(jnp.float32) - chosen.astype(jnp.float32)).astype(jnp.bfloat16)
    delta = lax.all_to_all(residual, "exp", split_axis=0, concat_axis=1, tiled=True)
    first = jnp.einsum("nrc,nck->nrk", delta, sketch, preferred_element_type=jnp.float32)
    return base, delta, [(((0, first.shape[1]),), sum_columns(first, col_size))]


def body(exp_size, col_size, weights, fisher, members, sketch):
    member_mask = members.astype(jnp.float32)
    folded = exp_size == 4 and weights.shape[1] == 24 * UNIT
    merge = merge_folded if folded else merge_spread
    base, delta, first = merge(weights, fisher, member_mask, sketch, col_size)
    side = lax.rem(lax.axis_index("col"), 2)[None]
    mine, others = sum_halves(*power_step(side, first, delta), col_size)
    basis, coeff = project(side, mine, others, delta)
    return base, basis, coeff


def solution(mesh):
    in_specs = (
        P(("grp", "exp"), None, "col"),
        P(("grp", "exp"), None),
        P("grp", None),
        P(("grp", "exp"), "col", None),
    )
    out_specs = (
        P("grp", "exp", "col"),
        P(("grp", "exp"), None, None),
        P(("grp", "exp"), None, "col"),
    )
    run = functools.partial(body, mesh.shape["exp"], mesh.shape["col"])
    return jax.shard_map(run, mesh=mesh, in_specs=in_specs, out_specs=out_specs, check_vma=False)
```

```python
import functools
import math

import jax
import jax.numpy as jnp
from jax import lax
from jax.experimental import pallas as pl
from jax.experimental.pallas import tpu as pltpu
from jax.sharding import PartitionSpec as P

HIGH = lax.Precision.HIGHEST
UNIT = 32
VMEM_LIMIT = 20 * 1024 * 1024
SMEM = pl.BlockSpec(memory_space=pltpu.SMEM)


def params():
    return pltpu.CompilerParams(vmem_limit_bytes=VMEM_LIMIT)


COST = pl.CostEstimate(flops=10**10, transcendentals=0, bytes_accessed=1)
ANY = pl.BlockSpec(memory_space=pl.ANY)
HBM = pl.BlockSpec(memory_space=pltpu.HBM)


def in_hbm(array):
    return pltpu.with_memory_space_constraint(array, pltpu.HBM)


def sums_kernel(ahead, inner, mask, w_ref, a_ref, f_ref, *refs):
    experts, rows, cols = w_ref.shape
    out_ref = refs[-2] if ahead else refs[-1]
    if ahead:

        @pl.when(inner[0] == 0)
        def _():
            refs[-1][...] = refs[0][...]

    @pl.when(inner[0] == 1)
    def _():
        clusters = out_ref.shape[0]
        strip, width = 16, 512
        across = cols // width

        def one(n, carry):
            r = pl.multiple_of((n // across) * strip, strip)
            c = pl.multiple_of((n % across) * width, width)
            at = (pl.ds(r, strip), pl.ds(c, width))
            totals = [jnp.zeros((strip, width), jnp.float32) for _ in range(clusters)]
            for e in range(2 * experts):
                source = w_ref if e < experts else a_ref
                block = source[e % experts, at[0], at[1]].astype(jnp.float32)
                block = block * f_ref[pl.ds(r, strip), e : e + 1]
                for k in range(clusters):
                    totals[k] = totals[k] + block * mask[e, k]
            for k in range(clusters):
                out_ref[k, at[0], at[1]] = totals[k].astype(jnp.bfloat16)
            return carry

        lax.fori_loop(0, (rows // strip) * across, one, 0)


def cluster_sums(inner, mask, weights, arrived, fcols, start, rows, ahead, after):
    experts, _, cols = weights.shape
    clusters = mask.shape[1]
    first = start // UNIT
    steps = rows // UNIT
    out_specs = [pl.BlockSpec((clusters, UNIT, cols), lambda i, on: (0, i * on[0], 0))]
    out_shape = [jax.ShapeDtypeStruct((clusters, rows, cols), jnp.bfloat16)]
    extra, extra_specs = list(after), [ANY] * len(after)
    if ahead is not None:
        begin, length = ahead
        split = length % (16 * steps) == 0 and begin % (length // steps) == 0
        part = length // steps if split else length
        shape = (experts, part, cols)
        if part != length:
            at = begin // part
            extra_specs.insert(0, pl.BlockSpec(shape, lambda i, on: (0, at + i * (1 - on[0]), 0)))
            out_specs.append(pl.BlockSpec(shape, lambda i, on: (0, i * (1 - on[0]), 0)))
        else:
            place = (pl.Element(experts), pl.Element(length), pl.Element(cols))
            extra_specs.insert(0, pl.BlockSpec(place, lambda i, on: (0, begin, 0)))
            out_specs.append(pl.BlockSpec(shape, lambda i, on: (0, 0, 0)))
        out_shape.append(jax.ShapeDtypeStruct((experts, length, cols), jnp.bfloat16))
        extra.insert(0, in_hbm(weights))
    return pl.pallas_call(
        functools.partial(sums_kernel, ahead is not None),
        grid_spec=pltpu.PrefetchScalarGridSpec(
            num_scalar_prefetch=1,
            grid=(steps,),
            in_specs=[
                SMEM,
                pl.BlockSpec((experts, UNIT, cols), lambda i, on: (0, first + i * on[0], 0)),
                pl.BlockSpec((experts, UNIT, cols), lambda i, on: (0, i * on[0], 0)),
                pl.BlockSpec((UNIT, fcols.shape[1]), lambda i, on: (first + i * on[0], 0)),
            ]
            + extra_specs,
            out_specs=out_specs,
        ),
        out_shape=out_shape,
        cost_estimate=COST,
        compiler_params=params(),
    )(inner, mask, in_hbm(weights), arrived, fcols, *extra)


def base_kernel(inner, labels, p_ref, q_ref, d_ref, *refs):
    clusters, rows, cols = p_ref.shape
    out_ref, chosen_ref = refs[-2:] if labels is not None else (refs[-1], None)

    @pl.when(inner[0] == 1)
    def _():
        scale = 1.0 / d_ref[...]
        for k in range(clusters):
            total = p_ref[k].astype(jnp.float32) + q_ref[k].astype(jnp.float32)
            out_ref[k] = (total * scale[:, k : k + 1]).astype(jnp.bfloat16)
        if chosen_ref is not None:
            for e in range(chosen_ref.shape[0]):
                chosen_ref[e] = out_ref[labels[e]]


def whole_base_kernel(inner, *refs):
    base_kernel(inner, None, *refs)


def make_base(inner, mine, other, denom, start, labels, after):
    clusters, rows, cols = mine.shape
    first = start // UNIT
    block = lambda lead: pl.BlockSpec((lead, UNIT, cols), lambda i, on: (0, i * on[0], 0))
    in_specs = [
        block(clusters),
        block(clusters),
        pl.BlockSpec((UNIT, clusters), lambda i, on: (first + i * on[0], 0)),
    ]
    shape = jax.ShapeDtypeStruct(mine.shape, jnp.bfloat16)
    kernel, operands, outs, shapes = whole_base_kernel, (), block(clusters), shape
    if labels is not None:
        kernel, operands = base_kernel, (labels,)
        in_specs = [SMEM] + in_specs
        experts = labels.shape[0]
        outs = [block(clusters), block(experts)]
        shapes = [shape, jax.ShapeDtypeStruct((experts, rows, cols), jnp.bfloat16)]
    return pl.pallas_call(
        kernel,
        grid_spec=pltpu.PrefetchScalarGridSpec(
            num_scalar_prefetch=1,
            grid=(rows // UNIT,),
            in_specs=in_specs + [ANY] * len(after),
            out_specs=outs,
        ),
        out_shape=shapes,
        cost_estimate=COST,
        compiler_params=params(),
    )(inner, *operands, mine, other, denom, *after)


def residual_kernel(meta, w_ref, b_ref, r_ref, s_ref, *refs):
    delta_ref, base_ref, first_ref = refs[-3:]
    experts = w_ref.shape[0]
    by_expert = r_ref.shape[0] == experts
    inner = meta[experts] == 1
    labels = [meta[e] for e in range(experts)]
    base_ref[...] = b_ref[...] if by_expert else r_ref[...]

    def subtract(source, indices):
        for e in range(experts):
            chosen = source[indices[e]].astype(jnp.float32)
            delta_ref[e] = (w_ref[e].astype(jnp.float32) - chosen).astype(jnp.bfloat16)

    @pl.when(inner)
    def _():
        subtract(b_ref, labels)

    @pl.when(jnp.logical_not(inner))
    def _():
        subtract(r_ref, range(experts) if by_expert else labels)

    for e in range(experts):
        first_ref[e] = jnp.dot(delta_ref[e], s_ref[e], preferred_element_type=jnp.float32)


def residual_chunk(meta, weights, base, arrived, sketch, quarter, start, held, after):
    experts, units, cols = weights.shape
    clusters, rows, _ = base.shape
    rank = sketch.shape[2]
    first = start // UNIT
    quarter_blocks = units // 4 // UNIT
    local = first - quarter * quarter_blocks
    own = lambda meta: meta[experts + 1] == quarter

    def keep(i, meta):
        return (0, jnp.where(own(meta), local + i, quarter_blocks), 0)

    chunk = lambda lead: pl.BlockSpec((lead, UNIT, cols), lambda i, meta: (0, i, 0))
    placed = pl.BlockSpec((experts, UNIT, cols), lambda i, meta: (0, first + i, 0))
    return pl.pallas_call(
        residual_kernel,
        grid_spec=pltpu.PrefetchScalarGridSpec(
            num_scalar_prefetch=1,
            grid=(rows // UNIT,),
            in_specs=[
                placed,
                chunk(clusters),
                chunk(arrived.shape[0]),
                pl.BlockSpec(sketch.shape, lambda i, meta: (0, 0, 0)),
            ]
            + [HBM] * len(held)
            + [ANY] * len(after),
            out_specs=[
                placed,
                pl.BlockSpec((clusters, UNIT, cols), keep),
                pl.BlockSpec((experts, UNIT, rank), lambda i, meta: (0, i, 0)),
            ],
        ),
        out_shape=[
            pltpu.HBM((experts, units, cols), jnp.bfloat16),
            pltpu.HBM((clusters, units // 4 + UNIT, cols), jnp.bfloat16),
            jax.ShapeDtypeStruct((experts, rows, rank), jnp.float32),
        ],
        cost_estimate=COST,
        input_output_aliases={5 + i: i for i in range(len(held))},
        compiler_params=params(),
    )(meta, in_hbm(weights), base, arrived, sketch, *held, *after)


def copy_kernel(in_ref, out_ref):
    out_ref[...] = in_ref[...]


def leading_rows(array, rows):
    lead, _, cols = array.shape
    block = pl.BlockSpec((lead, rows, cols // 2), lambda i: (0, 0, i))
    return pl.pallas_call(
        copy_kernel,
        grid=(2,),
        in_specs=[block],
        out_specs=block,
        out_shape=jax.ShapeDtypeStruct((lead, rows, cols), array.dtype),
        compiler_params=params(),
    )(array)


GROUP = 8


def inverse_factors(grams):
    size = grams[0].shape[0]
    lane = lax.broadcasted_iota(jnp.int32, (GROUP, size), 1)
    sub = lax.broadcasted_iota(jnp.int32, (GROUP, size), 0)
    groups = range(size // GROUP)
    tables = [[g[i * GROUP : (i + 1) * GROUP] for i in groups] for g in grams]
    for at in groups:
        first = at * GROUP
        block = (lane >= first) & (lane < first + GROUP)
        unit = jnp.where(lane - first == sub, 1.0, 0.0)
        for table in tables:
            own = table[at]
            cols = [
                jnp.broadcast_to(own[:, first + t : first + t + 1], (GROUP, size))
                for t in range(GROUP)
            ]
            rows = jnp.where(block, unit, own)
            diag = cols[0]
            for t in range(GROUP - 1):
                factor = jnp.where(sub > t, cols[t] * (1.0 / cols[t][t : t + 1]), 0.0)
                for s in range(t + 1, GROUP):
                    cols[s] = cols[s] - factor * cols[s][t : t + 1]
                rows = rows - factor * rows[t : t + 1]
                diag = jnp.where(sub > t, cols[t + 1], diag)
            inverse = 1.0 / diag
            table[at] = rows * lax.rsqrt(diag)
            solved = rows * inverse
            for t in range(GROUP - 1, 0, -1):
                upper = jnp.where(sub < t, cols[t] * inverse, 0.0)
                solved = solved - upper * solved[t : t + 1]
            for i in range(at + 1, size // GROUP):
                value = table[i]
                rest = jnp.where(block, 0.0, value)
                for t in range(GROUP):
                    col = jnp.broadcast_to(value[:, first + t : first + t + 1], (GROUP, size))
                    rest = rest - col * solved[t : t + 1]
                table[i] = rest
    out = []
    for table in tables:
        parts = [jnp.where(lane <= sub + i * GROUP, table[i], 0.0) for i in groups]
        out.append(jnp.concatenate(parts, axis=0))
    return out


def contract(left, right, dims, precision=None):
    return lax.dot_general(
        left, right, (dims, ((), ())), precision=precision, preferred_element_type=jnp.float32
    )


def ranges(values, units):
    grams = [contract(y, y, ((0,), (0,)), HIGH) for y in values]
    factors = inverse_factors(grams)
    return [
        (contract(y, m, ((1,), (1,)), HIGH) * math.sqrt(units)).astype(jnp.bfloat16)
        for y, m in zip(values, factors)
    ]


def power_kernel(splits, pieces, side, *refs):
    parts = refs[: sum(splits)]
    delta_ref = refs[sum(splits)]
    keep_ref, send_ref, value, held, sem = refs[-5:]
    experts, units, _ = delta_ref.shape
    half = units // 2
    copy = pltpu.make_async_copy(delta_ref, held, sem)
    copy.start()
    at = 0
    for count, places in zip(splits, pieces):
        total = parts[at][...].astype(jnp.float32)
        for part in parts[at + 1 : at + count]:
            total = total + part[...].astype(jnp.float32)
        row = 0
        for start, rows in places:
            value[:, start : start + rows] = total[:, row : row + rows]
            row += rows
        at = at + count
    start = ranges([value[e] for e in range(experts)], units)
    copy.wait()
    own = pl.multiple_of(side[0] * half, half)
    other = pl.multiple_of((1 - side[0]) * half, half)
    for e in range(experts):
        back = contract(start[e], held[e], ((0,), (0,))).astype(jnp.bfloat16)
        keep_ref[e] = contract(held[e, pl.ds(own, half)], back, ((1,), (1,)))
        send_ref[e] = contract(held[e, pl.ds(other, half)], back, ((1,), (1,))).astype(
            jnp.bfloat16
        )


def power_step(side, groups, delta):
    experts, units, _ = delta.shape
    pieces, groups = zip(*groups)
    rank = groups[0][0].shape[2]
    part = jax.ShapeDtypeStruct((experts, units // 2, rank), jnp.float32)
    vmem = pl.BlockSpec(memory_space=pltpu.VMEM)
    splits = tuple(len(g) for g in groups)
    return pl.pallas_call(
        functools.partial(power_kernel, splits, pieces),
        in_specs=[SMEM] + [vmem] * sum(splits) + [HBM],
        out_specs=[vmem] * 2,
        out_shape=[part, jax.ShapeDtypeStruct(part.shape, jnp.bfloat16)],
        scratch_shapes=[
            pltpu.VMEM((experts, units, rank), jnp.float32),
            pltpu.VMEM(delta.shape, jnp.bfloat16),
            pltpu.SemaphoreType.DMA,
        ],
        compiler_params=params(),
    )(side, *[term for g in groups for term in g], delta)


def project_kernel(side, *refs):
    parts, (delta_ref, basis_ref, coeff_ref, value, held, sem) = refs[:-6], refs[-6:]
    experts, half, _ = parts[0].shape
    units = 2 * half
    copy = pltpu.make_async_copy(delta_ref, held, sem)
    copy.start()
    count = len(parts) // 2
    for place, group in ((side[0], parts[:count]), (1 - side[0], parts[count:])):
        total = group[0][...].astype(jnp.float32)
        for part in group[1:]:
            total = total + part[...].astype(jnp.float32)
        value[:, pl.ds(pl.multiple_of(place * half, half), half)] = total
    basis = ranges([value[e] for e in range(experts)], units)
    copy.wait()
    for e in range(experts):
        basis_ref[e] = basis[e]
        coeff = contract(basis[e], held[e], ((0,), (0,)))
        coeff_ref[e] = (coeff * (1.0 / math.sqrt(units))).astype(jnp.bfloat16)


def project(side, mine, others, delta):
    experts, units, _ = delta.shape
    rank = mine[0].shape[2]
    vmem = pl.BlockSpec(memory_space=pltpu.VMEM)
    return pl.pallas_call(
        project_kernel,
        in_specs=[SMEM] + [vmem] * (len(mine) + len(others)) + [HBM],
        out_specs=[vmem] * 2,
        out_shape=[
            jax.ShapeDtypeStruct((experts, units, rank), jnp.bfloat16),
            jax.ShapeDtypeStruct((experts, rank, delta.shape[2]), jnp.bfloat16),
        ],
        scratch_shapes=[
            pltpu.VMEM((experts, units, rank), jnp.float32),
            pltpu.VMEM(delta.shape, jnp.bfloat16),
            pltpu.SemaphoreType.DMA,
        ],
        compiler_params=params(),
    )(side, *mine, *others, delta)


def swap(value, bit, size):
    return lax.ppermute(value, "col", [(i, i ^ bit) for i in range(size)])


def sum_columns(value, size):
    bit = 1
    while 2 * bit < size:
        value = value + swap(value, bit, size)
        bit *= 2
    value = value.astype(jnp.bfloat16)
    return value, swap(value, bit, size)


def sum_halves(keep, send, size):
    total = (keep + swap(send, 1, size).astype(jnp.float32)).astype(jnp.bfloat16)
    bit = 2
    while 2 * bit < size:
        total = (total.astype(jnp.float32) + swap(total, bit, size).astype(jnp.float32)).astype(
            jnp.bfloat16
        )
        bit *= 2
    far = swap(total, bit, size)
    return (total, far), (swap(total, 1, size), swap(far, 1, size))


def merge_folded(weights, fisher, member_mask, sketch, col_size):
    inwards, across, outwards = [(0, 1), (3, 2)], [(1, 2), (2, 1)], [(1, 0), (2, 3)]
    experts, units, cols = weights.shape
    clusters = member_mask.shape[1]
    place = lax.axis_index("exp")
    inner = ((place == 1) | (place == 2)).astype(jnp.int32)[None]
    mine = lax.dynamic_slice_in_dim(member_mask, place * experts, experts)
    partner = lax.dynamic_slice_in_dim(member_mask, (place ^ 1) * experts, experts)
    mask = jnp.concatenate([mine, partner], axis=0)
    meta = jnp.concatenate([jnp.argmax(mine, axis=1).astype(jnp.int32), inner, place[None]])
    opening = weights[:, : UNIT]
    fisher, opening = lax.optimization_barrier((fisher, opening))
    near = [fisher.astype(jnp.float32)]
    for hop in (1, 2, 3):
        pairs = [(i, i ^ hop) for i in range(4)]
        near.append(lax.ppermute(fisher, "exp", pairs).astype(jnp.float32))
    denom = jnp.zeros((units, clusters), jnp.float32)
    for hop, value in enumerate(near):
        rows = lax.dynamic_slice_in_dim(member_mask, (place ^ hop) * experts, experts)
        denom = denom + jnp.sum(value[:, :, None] * rows[:, None, :], axis=0)
    fcols = jnp.concatenate(near[:2], axis=0).T

    chunks = [(0, 1), (0, 2), (0, 3), (3, 3), (3, 3), (1, 3), (1, 3), (2, 3), (2, 2), (2, 1)]
    groups = [(0, 1, 2, 3, 4), (5, 6, 7), (8, 9)]
    lead, lag = 2, 2
    spans, used = [], [0] * 4
    for q, size in chunks:
        spans.append((q * (units // 4) + used[q], size * UNIT))
        used[q] += size * UNIT
    count = len(chunks)
    their_labels = jnp.argmax(partner, axis=1).astype(jnp.int32)
    arrived, sums, others, base, moved, firsts = {}, {}, {}, {}, {}, {}
    held, after, terms, ready = (), (), [], {}
    for c in range(lead):
        block = weights[:, spans[c][0] : sum(spans[c])] if c else opening
        arrived[c] = lax.ppermute(block, "exp", inwards)
    order = []
    for step in range(count):
        order += [("sums", step), ("base", step - 1), ("residual", step - lag)]
    order += [("base", count - 1)] + [("residual", c) for c in range(count - lag, count)]
    for kind, c in order:
        if c < 0:
            continue
        if kind == "sums":
            ahead = spans[c + lead] if c + lead < count else None
            sums[c], *copied = cluster_sums(
                inner, mask, weights, arrived[c], fcols, *spans[c], ahead, after
            )
            others[c] = lax.ppermute(sums[c], "exp", across)
            if copied:
                arrived[c + lead] = lax.ppermute(copied[0], "exp", inwards)
            after = (sums[c],)
        elif kind == "base":
            whole = chunks[c][0] in (0, 3)
            labels = None if whole else their_labels
            result = make_base(inner, sums[c], others[c], denom, spans[c][0], labels, after)
            base[c], leaving = (result, result) if whole else result
            moved[c] = lax.ppermute(leaving, "exp", outwards)
            after = (base[c],)
        else:
            if c == count - 2:
                after = after + (moved[count - 1],)
            *held, firsts[c] = residual_chunk(
                meta,
                weights,
                base[c],
                moved[c],
                sketch,
                chunks[c][0],
                spans[c][0],
                held,
                after + ready.pop(c, ()),
            )
            after = (firsts[c],)
            for group in groups:
                if c == group[-1]:
                    joined = jnp.concatenate([firsts[g] for g in group], axis=1)
                    total = sum_columns(joined, col_size)
                    terms.append((tuple(spans[g] for g in group), total))
                    ready[c + 2] = total[1:]
    delta, bases = held
    base = leading_rows(bases, units // 4)
    return base, delta, terms


def merge_spread(weights, fisher, member_mask, sketch, col_size):
    moved = lax.all_to_all(weights, "exp", split_axis=1, concat_axis=0, tiled=True)
    f_rows = lax.all_to_all(fisher, "exp", split_axis=1, concat_axis=0, tiled=True)
    f_wide = f_rows.astype(jnp.float32)
    weighted = f_wide[:, :, None] * moved.astype(jnp.float32)
    numer = jnp.einsum("ek,erc->krc", member_mask, weighted, precision=HIGH)
    denom = jnp.einsum("ek,er->kr", member_mask, f_wide, precision=HIGH)
    base = (numer / denom[:, :, None]).astype(jnp.bfloat16)
    chosen = jnp.take(base, jnp.argmax(member_mask, axis=1), axis=0)
    residual = (moved.astype(jnp.float32) - chosen.astype(jnp.float32)).astype(jnp.bfloat16)
    delta = lax.all_to_all(residual, "exp", split_axis=0, concat_axis=1, tiled=True)
    first = jnp.einsum("nrc,nck->nrk", delta, sketch, preferred_element_type=jnp.float32)
    return base, delta, [(((0, first.shape[1]),), sum_columns(first, col_size))]


def body(exp_size, col_size, weights, fisher, members, sketch):
    member_mask = members.astype(jnp.float32)
    folded = exp_size == 4 and weights.shape[1] == 24 * UNIT
    merge = merge_folded if folded else merge_spread
    base, delta, first = merge(weights, fisher, member_mask, sketch, col_size)
    side = lax.rem(lax.axis_index("col"), 2)[None]
    mine, others = sum_halves(*power_step(side, first, delta), col_size)
    basis, coeff = project(side, mine, others, delta)
    return base, basis, coeff


def solution(mesh):
    in_specs = (
        P(("grp", "exp"), None, "col"),
        P(("grp", "exp"), None),
        P("grp", None),
        P(("grp", "exp"), "col", None),
    )
    out_specs = (
        P("grp", "exp", "col"),
        P(("grp", "exp"), None, None),
        P(("grp", "exp"), None, "col"),
    )
    run = functools.partial(body, mesh.shape["exp"], mesh.shape["col"])
    return jax.shard_map(run, mesh=mesh, in_specs=in_specs, out_specs=out_specs, check_vma=False)
```
